1024 devices in a mesh: ep: 64 (over z, core), etp: 16 (over y, x).
Axes of the slice: x: 4, y: 4, z: 32, core: 2. Of those that a mesh axis runs over, the one named last changes fastest.
Arguments:
- tokens: bfloat16 [1024, 7168], P('ep', 'etp'), may hold values from -6 to 6
- grad_out: bfloat16 [1024, 7168], P('ep', 'etp'), may hold values from -6 to 6
- routes: int32 [1024, 8], P('ep'), may hold values from 0 to 31, all different within a row; in each aligned block of 16 rows (0 to 15, 16 to 31, ...) at most 5 rows name the same one
- route_gates: float32 [1024, 8], P('ep'), may hold values from 0.05 to 1
- gate_weight: bfloat16 [64, 3584, 2048], P('ep', None, 'etp'), may hold values from -0.0625 to 0.0625
- up_weight: bfloat16 [64, 3584, 2048], P('ep', None, 'etp'), may hold values from -0.0625 to 0.0625
- down_weight: bfloat16 [64, 2048, 3584], P('ep', 'etp'), may hold values from -0.125 to 0.125
Outputs:
- grad_tokens: bfloat16 [1024, 7168], P('ep', 'etp')
The draws below stay inside these ranges and needn't reach their ends.
Inputs may be any that keep to these rules, and one draw needn't show every extreme that they name: `routes`: each row names 8 different experts. In each aligned block of 16 rows (the tokens of one ep index) no expert is named by more than 5 rows, and in some block one expert is named by exactly 5 rows.
All inputs are finite; a program needn't handle non-finite values.
Results may differ from the reference program's by a relative error of at most 0.024.
Values may be sent and summed in bfloat16 or wider, within the bound.
No kernel may reach another device: no remote copies, remote signals or barrier semaphores. Data moves between devices by JAX's collectives and lax.ppermute only.
A program may use at most 32 MiB of HBM per device.

```python
import math
import jax
import jax.numpy as jnp
import numpy as np
from jax import lax

D = 7168
FF = 2048
GROUP = 16
TOKENS = 1024
EXPERTS = 32
TOPK = 8
CAP = 5
DQ = 224
N_EP = 64
N_ETP = 16


def block_scale(own_key, dims, pieces, low, largest):
    def one(dim, blocks):
        steps = jax.random.uniform(jax.random.fold_in(jax.random.fold_in(own_key, 6), dim), (blocks,), jnp.float32, low / len(pieces), largest / len(pieces))
        return jnp.repeat(jnp.exp(steps), dims[dim] // blocks).reshape((-1,) + (1,) * (len(dims) - dim - 1))

    gain = one(*pieces[0])
    for cut in pieces[1:]:
        gain = gain * one(*cut)
    return gain


def routed_block(rng, own, number, rows, amount, top, reach, slope):
    sequence = jax.random.permutation(rng, amount)
    packed, common = load_shares(amount, rows * top, reach, slope, True), load_shares(amount, rows * top, reach, slope, False)
    places = jnp.arange(amount)

    def named(tallies, turn):
        used = int((tallies > 0).sum())
        fixed = max(1, used // 4)
        shifted = fixed + (places - fixed + turn * (used - fixed)) % max(1, amount - fixed)
        return jnp.zeros((amount,), jnp.int32).at[sequence[jnp.where(places < fixed, places, shifted)]].set(jnp.asarray(tallies, jnp.int32))

    tallies = jnp.where(number % 4 == 0, named(packed, number // 4), named(common, number - number // 4 - 1))
    mixed = jax.random.permutation(jax.random.fold_in(own, 3), amount)
    donor, receiver = mixed[0:amount // 2 * 2:2], mixed[1:amount // 2 * 2:2]
    slack = jnp.minimum(tallies[donor] - 1, reach - tallies[receiver]) // 2
    slack = jnp.where((donor == sequence[0]) | (receiver == sequence[0]) | (tallies[receiver] == 0), 0, jnp.maximum(slack, 0))
    shifted = jax.random.randint(jax.random.fold_in(own, 4), (amount // 2,), 0, 1 << 20) % (slack + 1)
    tallies = tallies.at[donor].add(-shifted).at[receiver].add(shifted)
    labels = jnp.searchsorted(jnp.cumsum(tallies), jnp.arange(rows * top), side="right").astype(jnp.int32)
    grid = labels.reshape(top, rows).T
    grid = grid[jax.random.permutation(jax.random.fold_in(own, 1), rows)]
    turn = jax.random.randint(jax.random.fold_in(own, 2), (rows, 1), 0, top)
    return jnp.take_along_axis(grid, (jnp.arange(top)[None, :] + turn) % top, axis=1)


def load_shares(amount, total, reach, slope, full):
    weights = [(1 << 20) // math.isqrt(standing ** slope) + 1 for standing in range(1, amount + 1)]
    largest = reach if full else min(reach, max(-(-total // amount), total * weights[0] // sum(weights)))
    least = 1 if total - largest >= amount - 1 else 0
    given, rest = [largest] + [least] * (amount - 1), total - largest - least * (amount - 1)
    while rest > 0:
        candidates = [i for i in range(1, amount) if given[i] < largest] or [i for i in range(1, amount) if given[i] < reach]
        mass, budget = sum([weights[i] for i in candidates]), rest
        for i in candidates:
            extra = min(reach - given[i], max(1, budget * weights[i] // mass), rest)
            given[i] = given[i] + extra
            rest = rest - extra
    return np.array(given)


def scatter_about(rng, shape, width, limit, pieces=(), kind=jnp.bfloat16):
    drawn = width * jax.random.normal(rng, shape, jnp.float32)
    if pieces:
        drawn = drawn * block_scale(rng, shape, pieces, -0.22, 0.18)
    return jnp.clip(drawn, -limit, limit).astype(kind)


def setup_inputs(seed: int = 0) -> dict:
    key_of = jax.random.split(jax.random.key(seed), 8)
    tokens = scatter_about(key_of[0], (TOKENS, D), 1.0, 6.0, ((0, 64), (1, 16)))
    grad_out = scatter_about(key_of[1], (TOKENS, D), 1.0, 6.0, ((0, 64), (1, 16)))
    routes_keys = jax.random.split(jax.random.fold_in(key_of[2], 1), TOKENS // GROUP)
    routes_turns = jax.random.permutation(jax.random.fold_in(key_of[2], 3), TOKENS // GROUP)
    routes = jax.vmap(lambda own, number: routed_block(jax.random.fold_in(key_of[2], 2), own, number, GROUP, EXPERTS, TOPK, CAP, 2))(routes_keys, routes_turns).reshape((TOKENS, TOPK))
    route_gates = jnp.clip(jnp.exp(math.log(1.0) - 2.9957323 * jax.random.uniform(key_of[3], (TOKENS, TOPK), jnp.float32) ** block_scale(key_of[3], (TOKENS, TOPK), ((0, 64),), -0.2, 0.2)), 0.05, 1.0)
    gate_weight = scatter_about(key_of[4], (N_EP, D // 2, FF), D ** -0.5, 0.0625, ((0, 64), (2, 16)))
    up_weight = scatter_about(key_of[5], (N_EP, D // 2, FF), D ** -0.5, 0.0625, ((0, 64), (2, 16)))
    down_weight = scatter_about(key_of[6], (N_EP, FF, D // 2), FF ** -0.5, 0.125, ((0, 64), (1, 16)))
    return {"tokens": tokens, "grad_out": grad_out, "routes": routes, "route_gates": route_gates, "gate_weight": gate_weight, "up_weight": up_weight, "down_weight": down_weight}


def slot_tables(routes, route_gates):
    route_flat = routes.reshape(N_EP, GROUP * TOPK)
    gate_flat = route_gates.reshape(N_EP, GROUP * TOPK)
    expert_ids = jnp.arange(EXPERTS, dtype=jnp.int32)
    one_hot = (route_flat[:, :, None] == expert_ids[None, None, :]).astype(jnp.int32)
    earlier = jnp.cumsum(one_hot, axis=1) - one_hot
    route_rank = lax.optimization_barrier(jnp.sum(earlier * one_hot, axis=2)).astype(jnp.int32)
    slot_ids = jnp.arange(CAP, dtype=jnp.int32)
    chosen = (route_flat[:, None, None, :] == expert_ids[None, :, None, None]) & (route_rank[:, None, None, :] == slot_ids[None, None, :, None])
    owners = jnp.arange(N_EP, dtype=jnp.int32)[:, None] * GROUP + jnp.arange(GROUP * TOPK, dtype=jnp.int32)[None, :] // TOPK
    token_rows = lax.optimization_barrier(jnp.sum(jnp.where(chosen, owners[:, None, None, :], 0), axis=3)).astype(jnp.int32)
    filled = jnp.any(chosen, axis=3)
    scaled = lax.optimization_barrier(jnp.sum(jnp.where(chosen, gate_flat[:, None, None, :], 0.0), axis=3))

    def by_expert(table):
        return jnp.swapaxes(table, 0, 1).reshape(EXPERTS, N_EP * CAP)
    return (by_expert(token_rows), by_expert(filled), by_expert(scaled))

def assemble_rows(halves):
    return halves.reshape(2, N_ETP, DQ, FF).transpose(1, 0, 2, 3).reshape(D, FF)

def assemble_cols(halves):
    return halves.reshape(2, FF, N_ETP, DQ).transpose(1, 2, 0, 3).reshape(FF, D)

def reference(tokens, grad_out, routes, route_gates, gate_weight, up_weight, down_weight):
    token_rows, filled, scaled = slot_tables(routes, route_gates)
    expert_ids = jnp.arange(EXPERTS, dtype=jnp.int32)
    hidden_cols = FF // N_ETP
    rows_all = N_EP * CAP

    def expert_grad(operands):
        expert, rows_here, live, gate_here = operands
        inputs = jnp.where(live[:, None], tokens[rows_here], 0).astype(jnp.bfloat16)
        weighted = (gate_here[:, None] * grad_out[rows_here].astype(jnp.float32)).astype(jnp.bfloat16)
        start = (2 * expert).astype(jnp.int32)
        gate_full = assemble_rows(lax.dynamic_slice_in_dim(gate_weight, start, 2, 0))
        up_full = assemble_rows(lax.dynamic_slice_in_dim(up_weight, start, 2, 0))
        down_full = assemble_cols(lax.dynamic_slice_in_dim(down_weight, start, 2, 0))
        pre_gate = jnp.dot(inputs, gate_full, preferred_element_type=jnp.float32)
        pre_up = jnp.dot(inputs, up_full, preferred_element_type=jnp.float32)
        d_hidden = jnp.dot(weighted, down_full.T, preferred_element_type=jnp.float32)
        sigma = jax.nn.sigmoid(pre_gate)
        d_up = (d_hidden * pre_gate * sigma).astype(jnp.bfloat16)
        d_gate = (d_hidden * pre_up * sigma * (1.0 + pre_gate * (1.0 - sigma))).astype(jnp.bfloat16)
        gate_parts = jnp.einsum('rtf,dtf->trd', d_gate.astype(jnp.float32).reshape(rows_all, N_ETP, hidden_cols), gate_full.astype(jnp.float32).reshape(D, N_ETP, hidden_cols))
        up_parts = jnp.einsum('rtf,dtf->trd', d_up.astype(jnp.float32).reshape(rows_all, N_ETP, hidden_cols), up_full.astype(jnp.float32).reshape(D, N_ETP, hidden_cols))
        rounded = lax.optimization_barrier((gate_parts + up_parts).astype(jnp.bfloat16))
        return lax.optimization_barrier(jnp.sum(rounded.astype(jnp.float32), axis=0))
    grads = lax.map(expert_grad, (expert_ids, token_rows, filled, scaled))
    segments = jnp.where(filled, token_rows, TOKENS).reshape(EXPERTS * rows_all).astype(jnp.int32)
    total = jax.ops.segment_sum(grads.reshape(EXPERTS * rows_all, D), segments, num_segments=TOKENS + 1)
    return total[:TOKENS].astype(jnp.bfloat16)
```

```python
import functools

import jax
import jax.numpy as jnp
from jax import lax
from jax.experimental import pallas as pl
from jax.experimental.pallas import tpu as pltpu
from jax.sharding import PartitionSpec as P

SIDE = 4
STEPS = (0, 1, 3, 2)
NT = (((1,), (1,)), ((), ()))
NN = (((1,), (0,)), ((), ()))
VMEM_BYTES = 48 * 1024 * 1024


def mm(a, b, dims):
    return lax.dot_general(a, b, dims, preferred_element_type=jnp.float32)


def pack_kernel(gate_ref, up_ref, down_ref, o0, o1, o2, o3, sems):
    quarter = gate_ref.shape[0] // SIDE
    lanes = gate_ref.shape[1]
    chunks = quarter // lanes
    mine = lax.axis_index("etp") // SIDE
    copies = []

    def go(src, dst):
        copy = pltpu.make_async_copy(src, dst, sems.at[len(copies)])
        copy.start()
        copies.append(copy)

    for step, out in zip(STEPS, (o0, o1, o2, o3)):
        first = lax.rem(mine + step, SIDE) * quarter
        go(gate_ref.at[pl.ds(first, quarter)], out.at[pl.ds(0, quarter)])
        go(up_ref.at[pl.ds(first, quarter)], out.at[pl.ds(quarter, quarter)])
        for j in range(chunks):
            go(
                down_ref.at[:, pl.ds(pl.multiple_of(first + j * lanes, lanes), lanes)],
                out.at[pl.ds(2 * quarter + j * lanes, lanes)],
            )
    for copy in copies:
        copy.wait()


def pack_weights(gate, up, down):
    rows, lanes = gate.shape
    quarter = rows // SIDE
    shape = jax.ShapeDtypeStruct((3 * quarter, lanes), gate.dtype)
    count = SIDE * (2 + quarter // lanes)
    return pl.pallas_call(
        pack_kernel,
        out_shape=[shape] * SIDE,
        in_specs=[pl.BlockSpec(memory_space=pl.ANY)] * 3,
        out_specs=[pl.BlockSpec(memory_space=pl.ANY)] * SIDE,
        scratch_shapes=[pltpu.SemaphoreType.DMA((count,))],
        name="pack_weights",
    )(gate, up, down)


def forward_kernel(x_ref, w0, w1, w2, w3, out_ref):
    share = x_ref.shape[3]
    quarter = SIDE * share
    lanes = w0.shape[1]
    mine = lax.axis_index("etp") // SIDE
    for step, w in zip(STEPS, (w0, w1, w2, w3)):
        place = lax.rem(mine + step, SIDE)
        down = jnp.concatenate(
            [w[pl.ds(2 * quarter + j * lanes, lanes), :] for j in range(quarter // lanes)], axis=1
        )
        both = None
        hidden = None
        for x in range(SIDE):
            pair = jnp.concatenate(
                [w[pl.ds(x * share, share), :], w[pl.ds(quarter + x * share, share), :]], axis=1
            )
            one = mm(x_ref[x, 0], pair, NN)
            two = mm(x_ref[x, 1], down[:, x * share : (x + 1) * share], NT)
            both = one if both is None else both + one
            hidden = two if hidden is None else hidden + two
        out_ref[place, 0] = both[:, :lanes].astype(out_ref.dtype)
        out_ref[place, 1] = both[:, lanes:].astype(out_ref.dtype)
        out_ref[place, 2] = hidden.astype(out_ref.dtype)


def backward_kernel(d_ref, w0, w1, w2, w3, out_ref):
    share = out_ref.shape[2]
    quarter = SIDE * share
    mine = lax.axis_index("etp") // SIDE
    for x in range(SIDE):
        total = None
        for step, w in zip(STEPS, (w0, w1, w2, w3)):
            place = lax.rem(mine + step, SIDE)
            grads = jnp.concatenate([d_ref[place, 0], d_ref[place, 1]], axis=1)
            pair = jnp.concatenate(
                [w[pl.ds(x * share, share), :], w[pl.ds(quarter + x * share, share), :]], axis=1
            )
            one = mm(grads, pair, NT)
            total = one if total is None else total + one
        out_ref[x] = total.astype(out_ref.dtype)


def local_call(kernel, shape, count, flops, name):
    return pl.pallas_call(
        kernel,
        out_shape=jax.ShapeDtypeStruct(shape, jnp.bfloat16),
        in_specs=[pl.BlockSpec(memory_space=pltpu.VMEM)] * count,
        out_specs=pl.BlockSpec(memory_space=pltpu.VMEM),
        compiler_params=pltpu.CompilerParams(vmem_limit_bytes=VMEM_BYTES),
        cost_estimate=pl.CostEstimate(flops=flops, bytes_accessed=5_000_000, transcendentals=0),
        name=name,
    )


def on_device(tokens, grad_out, routes, route_gates, gate_weight, up_weight, down_weight):
    ep_count = lax.axis_size("ep")
    experts = ep_count // 2
    group_rows, top_count = routes.shape
    capacity = min(group_rows, 5 * group_rows * top_count // (4 * experts))
    half = tokens.shape[1] // 2
    rows_all = ep_count * capacity
    lanes = gate_weight.shape[2]
    along_x = [[SIDE * y + x for x in range(SIDE)] for y in range(SIDE)]
    along_y = [[SIDE * y + x for y in range(SIDE)] for x in range(SIDE)]

    packed = pack_weights(gate_weight[0], up_weight[0], down_weight[0])
    routes, route_gates, tokens, grad_out, *packed = lax.optimization_barrier(
        (routes, route_gates, tokens, grad_out, *packed)
    )
    weights = [packed[0]]
    for step, block in zip(STEPS[1:], packed[1:]):
        pairs = [
            (SIDE * y + x, SIDE * ((y + step) % SIDE) + x) for y in range(SIDE) for x in range(SIDE)
        ]
        weights.append(lax.ppermute(block, "etp", pairs))
    weights = [weights[0], weights[2], weights[1], weights[3]]

    expert_ids = jnp.arange(experts, dtype=jnp.int32)
    hit = routes[:, :, None] == expert_ids
    member = jnp.any(hit, axis=1).astype(jnp.int32)
    scale = jnp.sum(jnp.where(hit, route_gates[:, :, None], 0.0), axis=1)
    rank = jnp.cumsum(member, axis=0) - member
    slots = jnp.arange(capacity, dtype=jnp.int32)
    chosen = (member.T[:, None, :] == 1) & (rank.T[:, None, :] == slots[None, :, None])
    picker = chosen.astype(jnp.bfloat16)
    scaled = jnp.sum(jnp.where(chosen, scale.T[:, None, :], 0.0), axis=2)

    input_slots = jnp.einsum(
        "ecg,ghq->ehcq",
        picker,
        tokens.reshape(group_rows, 2, half),
        preferred_element_type=jnp.float32,
    ).astype(jnp.bfloat16)
    grad_slots = jnp.einsum(
        "ecg,ghq->ehcq",
        picker,
        grad_out.reshape(group_rows, 2, half),
        preferred_element_type=jnp.float32,
    )
    grad_slots = (grad_slots * scaled[:, None, :, None]).astype(jnp.bfloat16)
    sent = jnp.stack([input_slots, grad_slots], axis=2).reshape(ep_count, 2 * capacity * half)
    came = lax.all_to_all(sent, "ep", split_axis=0, concat_axis=0, tiled=True)
    rows = (
        came.reshape(ep_count, 2, capacity, half)
        .transpose(1, 0, 2, 3)
        .reshape(2, rows_all, half)
    )

    rows, *weights = lax.optimization_barrier((rows, *weights))
    wide = jnp.broadcast_to(rows[None], (SIDE, *rows.shape))
    gathered = lax.all_to_all(wide, "etp", 0, 0, tiled=True, axis_index_groups=along_x)
    flops = 2 * 3 * rows_all * half * SIDE * lanes * SIDE
    partial = local_call(
        forward_kernel, (SIDE, 3, rows_all, lanes), 5, flops, "forward_parts"
    )(gathered, *weights)
    partial = lax.all_to_all(partial, "etp", 0, 0, tiled=True, axis_index_groups=along_y)
    mine = jnp.sum(partial.astype(jnp.float32), axis=0)
    other = lax.ppermute(
        mine.astype(jnp.bfloat16), "ep", [(i, i ^ 1) for i in range(ep_count)]
    ).astype(jnp.float32)
    pre_gate, pre_up, d_hidden = mine + other
    sigma = jax.nn.sigmoid(pre_gate)
    d_up = (d_hidden * pre_gate * sigma).astype(jnp.bfloat16)
    d_gate = (d_hidden * pre_up * sigma * (1.0 + pre_gate * (1.0 - sigma))).astype(jnp.bfloat16)
    grads = lax.all_gather(jnp.stack([d_gate, d_up]), "etp", axis_index_groups=along_y)
    back = local_call(
        backward_kernel, (SIDE, rows_all, half), 5, flops * 2 // 3, "backward_parts"
    )(grads, *weights)
    back = lax.all_to_all(back, "etp", 0, 0, tiled=True, axis_index_groups=along_x)
    summed = jnp.sum(back.astype(jnp.float32), axis=0).astype(jnp.bfloat16)
    returned = lax.all_to_all(
        summed.reshape(ep_count, capacity * half), "ep", split_axis=0, concat_axis=0, tiled=True
    ).reshape(experts, 2, capacity, half)
    result = jnp.einsum(
        "ehcq,ecg->ghq", returned, picker, preferred_element_type=jnp.float32
    )
    return result.reshape(group_rows, 2 * half).astype(jnp.bfloat16)


def solution(mesh):
    return jax.shard_map(
        on_device,
        mesh=mesh,
        in_specs=(
            P("ep", "etp"),
            P("ep", "etp"),
            P("ep", None),
            P("ep", None),
            P("ep", None, "etp"),
            P("ep", None, "etp"),
            P("ep", "etp", None),
        ),
        out_specs=P("ep", "etp"),
        check_vma=False,
    )
```

```python
import jax
import jax.numpy as jnp
from jax import lax
from jax.experimental import pallas as pl
from jax.experimental.pallas import tpu as pltpu
from jax.sharding import PartitionSpec as P

SIDE = 4
STEPS = (0, 1, 3, 2)
NT = (((1,), (1,)), ((), ()))
NN = (((1,), (0,)), ((), ()))
TN = (((0,), (0,)), ((), ()))
LANES = 128
VMEM_BYTES = 48 * 1024 * 1024


def mm(a, b, dims, precision=None):
    return lax.dot_general(a, b, dims, precision=precision, preferred_element_type=jnp.float32)


def in_vmem(kernel, shapes, count, flops, name):
    return pl.pallas_call(
        kernel,
        out_shape=[jax.ShapeDtypeStruct(*shape) for shape in shapes],
        in_specs=[pl.BlockSpec(memory_space=pltpu.VMEM)] * count,
        out_specs=[pl.BlockSpec(memory_space=pltpu.VMEM)] * len(shapes),
        compiler_params=pltpu.CompilerParams(vmem_limit_bytes=VMEM_BYTES),
        cost_estimate=pl.CostEstimate(flops=flops, bytes_accessed=2_000_000, transcendentals=0),
        name=name,
    )


def pack_kernel(gate_ref, up_ref, down_ref, *outs):
    quarter = gate_ref.shape[0] // SIDE
    lanes = gate_ref.shape[1]
    mine = lax.axis_index("etp") // SIDE
    for step, out in zip(STEPS, outs):
        first = pl.multiple_of(lax.rem(mine + step, SIDE) * quarter, lanes)
        out[pl.ds(0, quarter), :] = gate_ref[pl.ds(first, quarter), :]
        out[pl.ds(quarter, quarter), :] = up_ref[pl.ds(first, quarter), :]
        for j in range(quarter // lanes):
            at = pl.multiple_of(first + j * lanes, lanes)
            out[pl.ds(2 * quarter + j * lanes, lanes), :] = down_ref[:, pl.ds(at, lanes)]


def dispatch_kernel(routes_ref, gates_ref, tokens_ref, grads_ref, inputs_out, grads_out, picks_out):
    group, top = routes_ref.shape
    capacity = picks_out.shape[0]
    width = picks_out.shape[2]
    sides = inputs_out.shape[0]
    half = tokens_ref.shape[1] // 2
    expert = lax.broadcasted_iota(jnp.int32, (group, width), 1) // 2
    member = jnp.zeros((group, width), jnp.float32)
    weight = jnp.zeros((group, width), jnp.float32)
    for k in range(top):
        named = expert == routes_ref[:, k : k + 1]
        member = jnp.where(named, 1.0, member)
        weight = jnp.where(named, gates_ref[:, k : k + 1], weight)
    earlier = lax.broadcasted_iota(jnp.int32, (group, group), 0) > lax.broadcasted_iota(
        jnp.int32, (group, group), 1
    )
    rank = mm(earlier.astype(jnp.float32), member, NN)
    even = lax.broadcasted_iota(jnp.int32, (width, half), 0) % 2 == 0
    tokens = tokens_ref[...].astype(jnp.float32)
    grads = grads_ref[...].astype(jnp.float32)
    input_parts, grad_parts = [], []
    for s in range(capacity):
        pick = jnp.where((rank > s - 0.5) & (rank < s + 0.5), member, 0.0)
        picks_out[s] = pick.astype(picks_out.dtype)
        one = mm(pick, tokens, TN)
        two = mm(pick * weight, grads, TN, lax.Precision.HIGHEST)
        input_parts.append(jnp.where(even, one[:, :half], one[:, half:]))
        grad_parts.append(jnp.where(even, two[:, :half], two[:, half:]))
    fill = jnp.zeros((width, inputs_out.shape[1] - capacity * half), jnp.float32)
    one = jnp.concatenate([*input_parts, fill], axis=1)[:sides]
    two = jnp.concatenate([*grad_parts, fill], axis=1)[:sides]
    inputs_out[...] = one.astype(inputs_out.dtype)
    grads_out[...] = two.astype(grads_out.dtype)


def spread_kernel(inputs_ref, grads_ref, out_ref):
    groups = inputs_ref.shape[0]
    half = out_ref.shape[3]
    for which, ref in enumerate((inputs_ref, grads_ref)):
        for s in range(out_ref.shape[2] // groups):
            block = ref[:, s * half : (s + 1) * half]
            for x in range(SIDE):
                out_ref[x, which, pl.ds(s * groups, groups), :] = block


def forward_kernel(x_ref, w0, w1, w2, w3, keep_ref, send_ref):
    share = x_ref.shape[3]
    quarter = SIDE * share
    lanes = w0.shape[1]
    rows = keep_ref.shape[2]
    mine = lax.axis_index("etp") // SIDE
    core = lax.rem(lax.axis_index("ep"), 2)
    for step, w in zip(STEPS, (w0, w1, w2, w3)):
        place = lax.rem(mine + step, SIDE)
        down = jnp.concatenate(
            [w[pl.ds(2 * quarter + j * lanes, lanes), :] for j in range(quarter // lanes)], axis=1
        )
        for out_ref, side in ((keep_ref, core), (send_ref, 1 - core)):
            here = pl.ds(pl.multiple_of(side * rows, 32), rows)
            both = None
            hidden = None
            for x in range(SIDE):
                pair = jnp.concatenate(
                    [w[pl.ds(x * share, share), :], w[pl.ds(quarter + x * share, share), :]],
                    axis=1,
                )
                one = mm(x_ref[x, 0, here, :], pair, NN)
                two = mm(x_ref[x, 1, here, :], down[:, x * share : (x + 1) * share], NT)
                both = one if both is None else both + one
                hidden = two if hidden is None else hidden + two
            out_ref[place, 0] = both[:, :lanes].astype(out_ref.dtype)
            out_ref[place, 1] = both[:, lanes:].astype(out_ref.dtype)
            out_ref[place, 2] = hidden.astype(out_ref.dtype)


def backward_kernel(d_ref, w0, w1, w2, w3, out_ref):
    share = out_ref.shape[2]
    rows = d_ref.shape[3]
    quarter = SIDE * share
    mine = lax.axis_index("etp") // SIDE
    for x in range(SIDE):
        for side in range(2):
            total = None
            for step, w in zip(STEPS, (w0, w1, w2, w3)):
                place = lax.rem(mine + step, SIDE)
                grads = jnp.concatenate([d_ref[side, place, 0], d_ref[side, place, 1]], axis=1)
                pair = jnp.concatenate(
                    [w[pl.ds(x * share, share), :], w[pl.ds(quarter + x * share, share), :]],
                    axis=1,
                )
                one = mm(grads, pair, NT)
                total = one if total is None else total + one
            out_ref[x, pl.ds(side * rows, rows), :] = total.astype(out_ref.dtype)


def gather_kernel(parts_ref, out_ref):
    groups = out_ref.shape[0]
    half = parts_ref.shape[2]
    capacity = parts_ref.shape[1] // groups
    blocks = []
    for s in range(capacity):
        here = pl.ds(s * groups, groups)
        total = parts_ref[0, here, :].astype(jnp.float32)
        for x in range(1, SIDE):
            total = total + parts_ref[x, here, :].astype(jnp.float32)
        blocks.append(total)
    blocks.append(jnp.zeros((groups, out_ref.shape[1] - capacity * half), jnp.float32))
    out_ref[...] = jnp.concatenate(blocks, axis=1).astype(out_ref.dtype)


def combine_kernel(came_ref, picks_ref, out_ref):
    sides = came_ref.shape[0]
    group = picks_ref.shape[1]
    half = out_ref.shape[1] // 2
    odd = lax.broadcasted_iota(jnp.int32, (group, sides), 1) % 2
    totals = [None, None]
    for s in range(picks_ref.shape[0]):
        block = came_ref[:, s * half : (s + 1) * half]
        pick = picks_ref[s].astype(jnp.float32)[:, :sides]
        for side in range(2):
            one = mm(jnp.where(odd == side, pick, 0.0).astype(block.dtype), block, NN)
            totals[side] = one if totals[side] is None else totals[side] + one
    out_ref[...] = jnp.concatenate(totals, axis=1).astype(out_ref.dtype)


def on_device(tokens, grad_out, routes, route_gates, gate_weight, up_weight, down_weight):
    bf16 = jnp.bfloat16
    ep_count = lax.axis_size("ep")
    experts = ep_count // 2
    group_rows, top_count = routes.shape
    capacity = min(group_rows, 5 * group_rows * top_count // (4 * experts))
    half = tokens.shape[1] // 2
    rows_all = ep_count * capacity
    lanes = gate_weight.shape[2]
    quarter = gate_weight.shape[1] // SIDE
    line = -(-capacity * half // LANES) * LANES
    back_line = -(-capacity * half // (2 * LANES)) * 2 * LANES
    along_x = [[SIDE * y + x for x in range(SIDE)] for y in range(SIDE)]
    along_y = [[SIDE * y + x for y in range(SIDE)] for x in range(SIDE)]
    cores = [[2 * z, 2 * z + 1] for z in range(experts)]

    packed = in_vmem(pack_kernel, [((3 * quarter, lanes), bf16)] * SIDE, 3, 0, "pack_weights")(
        gate_weight[0], up_weight[0], down_weight[0]
    )
    routes, route_gates, tokens, grad_out, *packed = lax.optimization_barrier(
        (routes, route_gates, tokens, grad_out, *packed)
    )
    weights = [packed[0]]
    for step, block in zip(STEPS[1:], packed[1:]):
        pairs = [
            (SIDE * y + x, SIDE * ((y + step) % SIDE) + x) for y in range(SIDE) for x in range(SIDE)
        ]
        weights.append(lax.ppermute(block, "etp", pairs))
    weights = [weights[0], weights[2], weights[1], weights[3]]

    sent_inputs, sent_grads, picks = in_vmem(
        dispatch_kernel,
        [
            ((ep_count, line), bf16),
            ((ep_count, line), bf16),
            ((capacity, group_rows, LANES), bf16),
        ],
        4,
        0,
        "dispatch_rows",
    )(routes, route_gates, tokens, grad_out)
    came = lax.all_to_all(
        jnp.stack([sent_inputs, sent_grads], axis=1), "ep", split_axis=0, concat_axis=0, tiled=True
    )
    came, *weights = lax.optimization_barrier((came, *weights))
    (wide,) = in_vmem(
        spread_kernel, [((SIDE, 2, rows_all, half), bf16)], 2, 0, "spread_rows"
    )(came[:, 0], came[:, 1])
    gathered = lax.all_to_all(wide, "etp", 0, 0, tiled=True, axis_index_groups=along_x)

    flops = 2 * 3 * rows_all * quarter * lanes * SIDE
    part = (SIDE, 3, rows_all // 2, lanes)
    keep, send = in_vmem(
        forward_kernel, [(part, jnp.float32), (part, bf16)], 5, flops, "forward_parts"
    )(gathered, *weights)
    other = lax.ppermute(send, "ep", [(i, i ^ 1) for i in range(ep_count)])
    partial = (keep + other.astype(jnp.float32)).astype(bf16)
    partial = lax.all_to_all(partial, "etp", 0, 0, tiled=True, axis_index_groups=along_y)
    pre_gate, pre_up, d_hidden = jnp.sum(partial.astype(jnp.float32), axis=0)
    sigma = jax.nn.sigmoid(pre_gate)
    d_up = (d_hidden * pre_gate * sigma).astype(bf16)
    d_gate = (d_hidden * pre_up * sigma * (1.0 + pre_gate * (1.0 - sigma))).astype(bf16)
    grads = lax.all_gather(jnp.stack([d_gate, d_up]), "etp", axis_index_groups=along_y)
    grads = lax.all_gather(grads, "ep", axis_index_groups=cores)
    (back,) = in_vmem(
        backward_kernel, [((SIDE, rows_all, half), bf16)], 5, flops * 2 // 3, "backward_parts"
    )(grads, *weights)
    back = lax.all_to_all(back, "etp", 0, 0, tiled=True, axis_index_groups=along_x)
    (summed,) = in_vmem(gather_kernel, [((ep_count, back_line), bf16)], 1, 0, "gather_rows")(back)
    returned = lax.all_to_all(summed, "ep", split_axis=0, concat_axis=0, tiled=True)
    (result,) = in_vmem(
        combine_kernel, [((group_rows, 2 * half), bf16)], 2, 0, "combine_rows"
    )(returned, picks)
    return result


def solution(mesh):
    return jax.shard_map(
        on_device,
        mesh=mesh,
        in_specs=(
            P("ep", "etp"),
            P("ep", "etp"),
            P("ep", None),
            P("ep", None),
            P("ep", None, "etp"),
            P("ep", None, "etp"),
            P("ep", "etp", None),
        ),
        out_specs=P("ep", "etp"),
        check_vma=False,
    )
```

```python
import jax
import jax.numpy as jnp
from jax import lax
from jax.experimental import pallas as pl
from jax.experimental.pallas import tpu as pltpu
from jax.sharding import PartitionSpec as P

SIDE = 4
STEPS = (0, 1, 3, 2)
NT = (((1,), (1,)), ((), ()))
NN = (((1,), (0,)), ((), ()))
TN = (((0,), (0,)), ((), ()))
LANES = 128
VMEM_BYTES = 48 * 1024 * 1024


def mm(a, b, dims, precision=None):
    return lax.dot_general(a, b, dims, precision=precision, preferred_element_type=jnp.float32)


def in_vmem(kernel, shapes, count, flops, name):
    return pl.pallas_call(
        kernel,
        out_shape=[jax.ShapeDtypeStruct(*shape) for shape in shapes],
        in_specs=[pl.BlockSpec(memory_space=pltpu.VMEM)] * count,
        out_specs=[pl.BlockSpec(memory_space=pltpu.VMEM)] * len(shapes),
        compiler_params=pltpu.CompilerParams(vmem_limit_bytes=VMEM_BYTES),
        cost_estimate=pl.CostEstimate(flops=flops, bytes_accessed=2_000_000, transcendentals=0),
        name=name,
    )


def pack_kernel(gate_ref, up_ref, down_ref, *rest):
    outs, sems = rest[:SIDE], rest[SIDE]
    quarter = gate_ref.shape[0] // SIDE
    lanes = gate_ref.shape[1]
    mine = lax.axis_index("etp") // SIDE
    copies = []
    for step, out in zip(STEPS, outs):
        first = pl.multiple_of(lax.rem(mine + step, SIDE) * quarter, lanes)
        pairs = [
            (gate_ref.at[pl.ds(first, quarter)], out.at[pl.ds(0, quarter)]),
            (up_ref.at[pl.ds(first, quarter)], out.at[pl.ds(quarter, quarter)]),
        ]
        for j in range(quarter // lanes):
            at = pl.multiple_of(first + j * lanes, lanes)
            pairs.append(
                (down_ref.at[:, pl.ds(at, lanes)], out.at[pl.ds(2 * quarter + j * lanes, lanes)])
            )
        for source, target in pairs:
            copy = pltpu.make_async_copy(source, target, sems.at[len(copies)])
            copy.start()
            copies.append(copy)
    for copy in copies:
        copy.wait()


def pack_weights(gate, up, down):
    quarter = gate.shape[0] // SIDE
    lanes = gate.shape[1]
    shape = jax.ShapeDtypeStruct((3 * quarter, lanes), gate.dtype)
    return pl.pallas_call(
        pack_kernel,
        out_shape=[shape] * SIDE,
        in_specs=[pl.BlockSpec(memory_space=pl.ANY)] * 3,
        out_specs=[pl.BlockSpec(memory_space=pltpu.VMEM)] * SIDE,
        scratch_shapes=[pltpu.SemaphoreType.DMA((SIDE * (2 + quarter // lanes),))],
        compiler_params=pltpu.CompilerParams(vmem_limit_bytes=VMEM_BYTES),
        cost_estimate=pl.CostEstimate(flops=0, bytes_accessed=6_000_000, transcendentals=0),
        name="pack_weights",
    )(gate, up, down)


def dispatch_kernel(routes_ref, gates_ref, tokens_ref, grads_ref, sent_out, picks_out):
    group, top = routes_ref.shape
    capacity = picks_out.shape[0]
    width = picks_out.shape[2]
    sides = sent_out.shape[0]
    half = tokens_ref.shape[1] // 2
    expert = lax.broadcasted_iota(jnp.int32, (group, width), 1) // 2
    member = jnp.zeros((group, width), jnp.float32)
    weight = jnp.zeros((group, width), jnp.float32)
    for k in range(top):
        named = expert == routes_ref[:, k : k + 1]
        member = jnp.where(named, 1.0, member)
        weight = jnp.where(named, gates_ref[:, k : k + 1], weight)
    earlier = lax.broadcasted_iota(jnp.int32, (group, group), 0) > lax.broadcasted_iota(
        jnp.int32, (group, group), 1
    )
    rank = mm(earlier.astype(jnp.float32), member, NN)
    even = lax.broadcasted_iota(jnp.int32, (width, half), 0) % 2 == 0
    tokens = tokens_ref[...].astype(jnp.float32)
    grads = grads_ref[...].astype(jnp.float32)
    input_parts, grad_parts = [], []
    for s in range(capacity):
        pick = jnp.where((rank > s - 0.5) & (rank < s + 0.5), member, 0.0)
        picks_out[s] = pick.astype(picks_out.dtype)
        one = mm(pick, tokens, TN)
        two = mm(pick * weight, grads, TN, lax.Precision.HIGHEST)
        input_parts.append(jnp.where(even, one[:, :half], one[:, half:]))
        grad_parts.append(jnp.where(even, two[:, :half], two[:, half:]))
    fill = jnp.zeros((width, sent_out.shape[2] - capacity * half), jnp.float32)
    one = jnp.concatenate([*input_parts, fill], axis=1)[:sides]
    two = jnp.concatenate([*grad_parts, fill], axis=1)[:sides]
    sent_out[:, 0, :] = one.astype(sent_out.dtype)
    sent_out[:, 1, :] = two.astype(sent_out.dtype)


def spread_kernel(inputs_ref, grads_ref, out_ref):
    groups = inputs_ref.shape[0]
    half = out_ref.shape[3]
    for which, ref in enumerate((inputs_ref, grads_ref)):
        for s in range(out_ref.shape[2] // groups):
            block = ref[:, s * half : (s + 1) * half]
            for x in range(SIDE):
                out_ref[x, which, pl.ds(s * groups, groups), :] = block


def forward_kernel(x_ref, w0, w1, w2, w3, keep_ref, send_ref):
    share = x_ref.shape[3]
    quarter = SIDE * share
    lanes = w0.shape[1]
    rows = keep_ref.shape[2]
    mine = lax.axis_index("etp") // SIDE
    core = lax.rem(lax.axis_index("ep"), 2)
    for step, w in zip(STEPS, (w0, w1, w2, w3)):
        place = lax.rem(mine + step, SIDE)
        down = jnp.concatenate(
            [w[pl.ds(2 * quarter + j * lanes, lanes), :] for j in range(quarter // lanes)], axis=1
        )
        for out_ref, side in ((keep_ref, core), (send_ref, 1 - core)):
            here = pl.ds(pl.multiple_of(side * rows, 32), rows)
            both = None
            hidden = None
            for x in range(SIDE):
                pair = jnp.concatenate(
                    [w[pl.ds(x * share, share), :], w[pl.ds(quarter + x * share, share), :]],
                    axis=1,
                )
                one = mm(x_ref[x, 0, here, :], pair, NN)
                two = mm(x_ref[x, 1, here, :], down[:, x * share : (x + 1) * share], NT)
                both = one if both is None else both + one
                hidden = two if hidden is None else hidden + two
            out_ref[place, 0] = both[:, :lanes].astype(out_ref.dtype)
            out_ref[place, 1] = both[:, lanes:].astype(out_ref.dtype)
            out_ref[place, 2] = hidden.astype(out_ref.dtype)


def backward_kernel(d_ref, w0, w1, w2, w3, out_ref):
    share = out_ref.shape[2]
    quarter = SIDE * share
    mine = lax.axis_index("etp") // SIDE
    grads = []
    for step in STEPS:
        place = lax.rem(mine + step, SIDE)
        grads.append(
            jnp.concatenate(
                [
                    jnp.concatenate([d_ref[side, place, 0], d_ref[side, place, 1]], axis=1)
                    for side in range(2)
                ],
                axis=0,
            )
        )
    for x in range(SIDE):
        total = None
        for grad, w in zip(grads, (w0, w1, w2, w3)):
            pair = jnp.concatenate(
                [w[pl.ds(x * share, share), :], w[pl.ds(quarter + x * share, share), :]], axis=1
            )
            one = mm(grad, pair, NT)
            total = one if total is None else total + one
        out_ref[x] = total.astype(out_ref.dtype)


def gather_kernel(parts_ref, out_ref):
    groups = out_ref.shape[0]
    width = out_ref.shape[2]
    half = parts_ref.shape[2]
    capacity = parts_ref.shape[1] // groups
    blocks = []
    for s in range(capacity):
        here = pl.ds(s * groups, groups)
        total = parts_ref[0, here, :].astype(jnp.float32)
        for x in range(1, SIDE):
            total = total + parts_ref[x, here, :].astype(jnp.float32)
        blocks.append(total)
    blocks.append(jnp.zeros((groups, 2 * width - capacity * half), jnp.float32))
    line = jnp.concatenate(blocks, axis=1).astype(out_ref.dtype)
    out_ref[:, 0, :] = line[:, :width]
    out_ref[:, 1, :] = line[:, width:]


def combine_kernel(came_ref, picks_ref, out_ref):
    sides = came_ref.shape[0]
    group = picks_ref.shape[1]
    half = out_ref.shape[1] // 2
    odd = lax.broadcasted_iota(jnp.int32, (group, sides), 1) % 2
    totals = [None, None]
    for s in range(picks_ref.shape[0]):
        block = came_ref[:, s * half : (s + 1) * half]
        pick = picks_ref[s].astype(jnp.float32)[:, :sides]
        for side in range(2):
            one = mm(jnp.where(odd == side, pick, 0.0).astype(block.dtype), block, NN)
            totals[side] = one if totals[side] is None else totals[side] + one
    out_ref[...] = jnp.concatenate(totals, axis=1).astype(out_ref.dtype)


def on_device(tokens, grad_out, routes, route_gates, gate_weight, up_weight, down_weight):
    bf16 = jnp.bfloat16
    ep_count = lax.axis_size("ep")
    experts = ep_count // 2
    group_rows, top_count = routes.shape
    capacity = min(group_rows, 5 * group_rows * top_count // (4 * experts))
    half = tokens.shape[1] // 2
    rows_all = ep_count * capacity
    lanes = gate_weight.shape[2]
    quarter = gate_weight.shape[1] // SIDE
    line = -(-capacity * half // LANES) * LANES
    back_line = -(-capacity * half // (2 * LANES)) * 2 * LANES
    along_x = [[SIDE * y + x for x in range(SIDE)] for y in range(SIDE)]
    along_y = [[SIDE * y + x for y in range(SIDE)] for x in range(SIDE)]
    cores = [[2 * z, 2 * z + 1] for z in range(experts)]

    packed = pack_weights(gate_weight[0], up_weight[0], down_weight[0])
    weights = [packed[0]]
    for step, block in zip(STEPS[1:], packed[1:]):
        pairs = [
            (SIDE * y + x, SIDE * ((y + step) % SIDE) + x) for y in range(SIDE) for x in range(SIDE)
        ]
        weights.append(lax.ppermute(block, "etp", pairs))
    weights = [weights[0], weights[2], weights[1], weights[3]]

    sent, picks = in_vmem(
        dispatch_kernel,
        [
            ((ep_count, 2, line), bf16),
            ((capacity, group_rows, LANES), bf16),
        ],
        4,
        0,
        "dispatch_rows",
    )(routes, route_gates, tokens, grad_out)
    came = lax.all_to_all(sent, "ep", split_axis=0, concat_axis=0, tiled=True)
    came, *weights = lax.optimization_barrier((came, *weights))
    (wide,) = in_vmem(
        spread_kernel, [((SIDE, 2, rows_all, half), bf16)], 2, 0, "spread_rows"
    )(came[:, 0], came[:, 1])
    gathered = lax.all_to_all(wide, "etp", 0, 0, tiled=True, axis_index_groups=along_x)

    flops = 2 * 3 * rows_all * quarter * lanes * SIDE
    part = (SIDE, 3, rows_all // 2, lanes)
    keep, send = in_vmem(
        forward_kernel, [(part, jnp.float32), (part, bf16)], 5, flops, "forward_parts"
    )(gathered, *weights)
    other = lax.ppermute(send, "ep", [(i, i ^ 1) for i in range(ep_count)])
    partial = (keep + other.astype(jnp.float32)).astype(bf16)
    partial = lax.all_to_all(partial, "etp", 0, 0, tiled=True, axis_index_groups=along_y)
    pre_gate, pre_up, d_hidden = jnp.sum(partial.astype(jnp.float32), axis=0)
    sigma = jax.nn.sigmoid(pre_gate)
    d_up = (d_hidden * pre_gate * sigma).astype(bf16)
    d_gate = (d_hidden * pre_up * sigma * (1.0 + pre_gate * (1.0 - sigma))).astype(bf16)
    grads = jnp.broadcast_to(jnp.stack([d_gate, d_up])[None], (SIDE, 2, *d_up.shape))
    grads = lax.all_to_all(grads, "etp", 0, 0, tiled=True, axis_index_groups=along_y)
    grads = lax.all_gather(grads, "ep", axis_index_groups=cores)
    (back,) = in_vmem(
        backward_kernel, [((SIDE, rows_all, half), bf16)], 5, flops * 2 // 3, "backward_parts"
    )(grads, *weights)
    back = lax.all_to_all(back, "etp", 0, 0, tiled=True, axis_index_groups=along_x)
    (summed,) = in_vmem(gather_kernel, [((ep_count, 2, back_line // 2), bf16)], 1, 0, "gather_rows")(back)
    returned = lax.all_to_all(summed, "ep", split_axis=0, concat_axis=0, tiled=True)
    (result,) = in_vmem(
        combine_kernel, [((group_rows, 2 * half), bf16)], 2, 0, "combine_rows"
    )(returned.reshape(ep_count, back_line), picks)
    return result


def solution(mesh):
    return jax.shard_map(
        on_device,
        mesh=mesh,
        in_specs=(
            P("ep", "etp"),
            P("ep", "etp"),
            P("ep", None),
            P("ep", None),
            P("ep", None, "etp"),
            P("ep", None, "etp"),
            P("ep", "etp", None),
        ),
        out_specs=P("ep", "etp"),
        check_vma=False,
    )
```

```python
import jax
import jax.numpy as jnp
from jax import lax
from jax.experimental import pallas as pl
from jax.experimental.pallas import tpu as pltpu
from jax.sharding import PartitionSpec as P

SIDE = 4
STEPS = (0, 1, 3, 2)
NT = (((1,), (1,)), ((), ()))
NN = (((1,), (0,)), ((), ()))
TN = (((0,), (0,)), ((), ()))
LANES = 128
VMEM_BYTES = 48 * 1024 * 1024


def mm(a, b, dims, precision=None):
    return lax.dot_general(a, b, dims, precision=precision, preferred_element_type=jnp.float32)


def in_vmem(kernel, shapes, count, flops, name):
    return pl.pallas_call(
        kernel,
        out_shape=[jax.ShapeDtypeStruct(*shape) for shape in shapes],
        in_specs=[pl.BlockSpec(memory_space=pltpu.VMEM)] * count,
        out_specs=[pl.BlockSpec(memory_space=pltpu.VMEM)] * len(shapes),
        compiler_params=pltpu.CompilerParams(vmem_limit_bytes=VMEM_BYTES),
        cost_estimate=pl.CostEstimate(flops=flops, bytes_accessed=2_000_000, transcendentals=0),
        name=name,
    )


def start_kernel(routes_any, gates_any, tokens_any, grads_any, gate_any, up_any, down_any, *rest):
    sent_out, picks_out = rest[:2]
    own, ahead, behind, far_low, far_high = rest[2:7]
    routes_ref, gates_ref, tokens_ref, grads_ref, small_sems, sems = rest[7:]
    quarter = gate_any.shape[0] // SIDE
    lanes = gate_any.shape[1]
    small = []
    for which, (source, target) in enumerate(
        (
            (routes_any, routes_ref),
            (gates_any, gates_ref),
            (tokens_any, tokens_ref),
            (grads_any, grads_ref),
        )
    ):
        copy = pltpu.make_async_copy(source, target, small_sems.at[which])
        copy.start()
        small.append(copy)
    mine = lax.axis_index("etp") // SIDE
    copies = []

    def go(source, target):
        copy = pltpu.make_async_copy(source, target, sems.at[len(copies)])
        copy.start()
        copies.append(copy)

    for step, outs in ((2, (far_low, far_high)), (1, (ahead,)), (3, (behind,)), (0, (own,))):
        first = pl.multiple_of(lax.rem(mine + step, SIDE) * quarter, lanes)
        cut = outs[0].shape[0] - quarter
        go(gate_any.at[pl.ds(first, quarter)], outs[0].at[pl.ds(0, quarter)])
        if len(outs) == 1:
            go(up_any.at[pl.ds(first, quarter)], outs[0].at[pl.ds(quarter, quarter)])
            base = 2 * quarter
        else:
            go(up_any.at[pl.ds(first, cut)], outs[0].at[pl.ds(quarter, cut)])
            go(up_any.at[pl.ds(first + cut, quarter - cut)], outs[1].at[pl.ds(0, quarter - cut)])
            base = quarter - cut
        for j in range(quarter // lanes):
            at = pl.multiple_of(first + j * lanes, lanes)
            go(down_any.at[:, pl.ds(at, lanes)], outs[-1].at[pl.ds(base + j * lanes, lanes)])

    for copy in small:
        copy.wait()
    top, group = routes_ref.shape
    capacity, sides, _ = picks_out.shape
    half = tokens_ref.shape[1] // 2
    expert = lax.broadcasted_iota(jnp.int32, (sides, group), 0) // 2
    member = jnp.zeros((sides, group), jnp.float32)
    weight = jnp.zeros((sides, group), jnp.float32)
    for k in range(top):
        named = expert == routes_ref[k : k + 1, :]
        member = jnp.where(named, 1.0, member)
        weight = jnp.where(named, gates_ref[k : k + 1, :], weight)
    earlier = lax.broadcasted_iota(jnp.int32, (group, group), 0) < lax.broadcasted_iota(
        jnp.int32, (group, group), 1
    )
    rank = mm(member, earlier.astype(jnp.float32), NN)
    even = lax.broadcasted_iota(jnp.int32, (sides, half), 0) % 2 == 0
    tokens = tokens_ref[...].astype(jnp.float32)
    grads = grads_ref[...].astype(jnp.float32)
    input_parts, grad_parts = [], []
    for s in range(capacity):
        pick = jnp.where((rank > s - 0.5) & (rank < s + 0.5), member, 0.0)
        picks_out[s] = pick
        one = mm(pick, tokens, NN)
        two = mm(pick * weight, grads, NN, lax.Precision.HIGHEST)
        input_parts.append(jnp.where(even, one[:, :half], one[:, half:]))
        grad_parts.append(jnp.where(even, two[:, :half], two[:, half:]))
    fill = jnp.zeros((sides, sent_out.shape[2] - capacity * half), jnp.float32)
    sent_out[:, 0, :] = jnp.concatenate([*input_parts, fill], axis=1).astype(sent_out.dtype)
    sent_out[:, 1, :] = jnp.concatenate([*grad_parts, fill], axis=1).astype(sent_out.dtype)
    for copy in copies:
        copy.wait()


def start(routes, gates, tokens, grads, gate, up, down, capacity, sides, line):
    quarter = gate.shape[0] // SIDE
    lanes = gate.shape[1]
    whole = jax.ShapeDtypeStruct((3 * quarter, lanes), gate.dtype)
    part = jax.ShapeDtypeStruct((3 * quarter // 2, lanes), gate.dtype)
    shapes = [
        jax.ShapeDtypeStruct((sides, 2, line), tokens.dtype),
        jax.ShapeDtypeStruct((capacity, sides, routes.shape[1]), jnp.float32),
        whole,
        whole,
        whole,
        part,
        part,
    ]
    small = (routes, gates, tokens, grads)
    return pl.pallas_call(
        start_kernel,
        out_shape=shapes,
        in_specs=[pl.BlockSpec(memory_space=pl.ANY)] * 7,
        out_specs=[pl.BlockSpec(memory_space=pltpu.VMEM)] * len(shapes),
        scratch_shapes=[
            *[pltpu.VMEM(array.shape, array.dtype) for array in small],
            pltpu.SemaphoreType.DMA((len(small),)),
            pltpu.SemaphoreType.DMA((SIDE * (2 + quarter // lanes) + 1,)),
        ],
        compiler_params=pltpu.CompilerParams(vmem_limit_bytes=60 * 1024 * 1024),
        cost_estimate=pl.CostEstimate(flops=0, bytes_accessed=6_000_000, transcendentals=0),
        name="start_rows",
    )(*small, gate, up, down)


def rows_of(parts, first, count):
    for part in parts:
        if first < part.shape[0]:
            return part[pl.ds(first, count), :]
        first -= part.shape[0]
    return None


def spread_kernel(inputs_ref, grads_ref, out_ref):
    groups = inputs_ref.shape[0]
    half = out_ref.shape[3]
    for which, ref in enumerate((inputs_ref, grads_ref)):
        for s in range(out_ref.shape[2] // groups):
            block = ref[:, s * half : (s + 1) * half]
            for x in range(SIDE):
                out_ref[x, which, pl.ds(s * groups, groups), :] = block


def forward_kernel(x_ref, own, ahead, behind, far_low, far_high, keep_ref, send_ref):
    share = x_ref.shape[3]
    quarter = SIDE * share
    lanes = own.shape[1]
    rows = keep_ref.shape[2]
    mine = lax.axis_index("etp") // SIDE
    core = lax.rem(lax.axis_index("ep"), 2)
    for step, w in zip(STEPS, ((own,), (ahead,), (behind,), (far_low, far_high))):
        place = lax.rem(mine + step, SIDE)
        down = jnp.concatenate(
            [rows_of(w, 2 * quarter + j * lanes, lanes) for j in range(quarter // lanes)], axis=1
        )
        for out_ref, side in ((keep_ref, core), (send_ref, 1 - core)):
            here = pl.ds(pl.multiple_of(side * rows, 32), rows)
            both = None
            hidden = None
            for x in range(SIDE):
                pair = jnp.concatenate(
                    [rows_of(w, x * share, share), rows_of(w, quarter + x * share, share)],
                    axis=1,
                )
                one = mm(x_ref[x, 0, here, :], pair, NN)
                two = mm(x_ref[x, 1, here, :], down[:, x * share : (x + 1) * share], NT)
                both = one if both is None else both + one
                hidden = two if hidden is None else hidden + two
            out_ref[place, 0] = both[:, :lanes].astype(out_ref.dtype)
            out_ref[place, 1] = both[:, lanes:].astype(out_ref.dtype)
            out_ref[place, 2] = hidden.astype(out_ref.dtype)


def backward_kernel(d_ref, own, ahead, behind, far_low, far_high, out_ref):
    share = out_ref.shape[2]
    quarter = SIDE * share
    mine = lax.axis_index("etp") // SIDE
    grads = []
    for step in STEPS:
        place = lax.rem(mine + step, SIDE)
        grads.append(
            jnp.concatenate(
                [
                    jnp.concatenate([d_ref[side, place, 0], d_ref[side, place, 1]], axis=1)
                    for side in range(2)
                ],
                axis=0,
            )
        )
    for x in range(SIDE):
        total = None
        for grad, w in zip(grads, ((own,), (ahead,), (behind,), (far_low, far_high))):
            pair = jnp.concatenate(
                [rows_of(w, x * share, share), rows_of(w, quarter + x * share, share)], axis=1
            )
            one = mm(grad, pair, NT)
            total = one if total is None else total + one
        out_ref[x] = total.astype(out_ref.dtype)


def gather_kernel(parts_ref, out_ref):
    groups = out_ref.shape[0]
    width = out_ref.shape[2]
    half = parts_ref.shape[2]
    capacity = parts_ref.shape[1] // groups
    blocks = []
    for s in range(capacity):
        here = pl.ds(s * groups, groups)
        total = parts_ref[0, here, :].astype(jnp.float32)
        for x in range(1, SIDE):
            total = total + parts_ref[x, here, :].astype(jnp.float32)
        blocks.append(total)
    blocks.append(jnp.zeros((groups, 2 * width - capacity * half), jnp.float32))
    line = jnp.concatenate(blocks, axis=1).astype(out_ref.dtype)
    out_ref[:, 0, :] = line[:, :width]
    out_ref[:, 1, :] = line[:, width:]


def combine_kernel(came_ref, picks_ref, out_ref):
    capacity, sides, group = picks_ref.shape
    half = out_ref.shape[1] // 2
    odd = lax.broadcasted_iota(jnp.int32, (sides, group), 0) % 2
    totals = [None, None]
    for s in range(capacity):
        block = came_ref[:, s * half : (s + 1) * half].astype(jnp.float32)
        for side in range(2):
            one = mm(jnp.where(odd == side, picks_ref[s], 0.0), block, TN)
            totals[side] = one if totals[side] is None else totals[side] + one
    out_ref[...] = jnp.concatenate(totals, axis=1).astype(out_ref.dtype)


def on_device(tokens, grad_out, routes, route_gates, gate_weight, up_weight, down_weight):
    bf16 = jnp.bfloat16
    ep_count = lax.axis_size("ep")
    experts = ep_count // 2
    group_rows, top_count = routes.shape
    capacity = min(group_rows, 5 * group_rows * top_count // (4 * experts))
    half = tokens.shape[1] // 2
    rows_all = ep_count * capacity
    lanes = gate_weight.shape[2]
    quarter = gate_weight.shape[1] // SIDE
    line = -(-capacity * half // LANES) * LANES
    back_line = -(-capacity * half // (2 * LANES)) * 2 * LANES
    along_x = [[SIDE * y + x for x in range(SIDE)] for y in range(SIDE)]
    along_y = [[SIDE * y + x for y in range(SIDE)] for x in range(SIDE)]
    cores = [[2 * z, 2 * z + 1] for z in range(experts)]

    sent, picks, own, to_ahead, to_behind, to_far_low, to_far_high = start(
        routes.T,
        route_gates.T,
        tokens,
        grad_out,
        gate_weight[0],
        up_weight[0],
        down_weight[0],
        capacity,
        ep_count,
        line,
    )

    def shift(block, step):
        pairs = [
            (SIDE * y + x, SIDE * ((y + step) % SIDE) + x) for y in range(SIDE) for x in range(SIDE)
        ]
        return lax.ppermute(block, "etp", pairs)

    far_low = shift(shift(to_far_low, 1), 1)
    far_high = shift(shift(to_far_high, -1), -1)
    weights = [own, shift(to_behind, -1), shift(to_ahead, 1), far_low, far_high]

    came = lax.all_to_all(sent, "ep", split_axis=0, concat_axis=0, tiled=True)
    came, *weights = lax.optimization_barrier((came, *weights))
    (wide,) = in_vmem(
        spread_kernel, [((SIDE, 2, rows_all, half), bf16)], 2, 0, "spread_rows"
    )(came[:, 0], came[:, 1])
    gathered = lax.all_to_all(wide, "etp", 0, 0, tiled=True, axis_index_groups=along_x)

    flops = 2 * 3 * rows_all * quarter * lanes * SIDE
    part = (SIDE, 3, rows_all // 2, lanes)
    keep, send = in_vmem(
        forward_kernel, [(part, jnp.float32), (part, bf16)], 6, flops, "forward_parts"
    )(gathered, *weights)
    other = lax.ppermute(send, "ep", [(i, i ^ 1) for i in range(ep_count)])
    partial = (keep + other.astype(jnp.float32)).astype(bf16)
    partial = lax.all_to_all(partial, "etp", 0, 0, tiled=True, axis_index_groups=along_y)
    pre_gate, pre_up, d_hidden = jnp.sum(partial.astype(jnp.float32), axis=0)
    sigma = jax.nn.sigmoid(pre_gate)
    d_up = (d_hidden * pre_gate * sigma).astype(bf16)
    d_gate = (d_hidden * pre_up * sigma * (1.0 + pre_gate * (1.0 - sigma))).astype(bf16)
    grads = jnp.broadcast_to(jnp.stack([d_gate, d_up])[None], (SIDE, 2, *d_up.shape))
    grads = lax.all_to_all(grads, "etp", 0, 0, tiled=True, axis_index_groups=along_y)
    grads = lax.all_gather(grads, "ep", axis_index_groups=cores)
    (back,) = in_vmem(
        backward_kernel, [((SIDE, rows_all, half), bf16)], 6, flops * 2 // 3, "backward_parts"
    )(grads, *weights)
    back = lax.all_to_all(back, "etp", 0, 0, tiled=True, axis_index_groups=along_x)
    (summed,) = in_vmem(gather_kernel, [((ep_count, 2, back_line // 2), bf16)], 1, 0, "gather_rows")(back)
    returned = lax.all_to_all(summed, "ep", split_axis=0, concat_axis=0, tiled=True)
    (result,) = in_vmem(
        combine_kernel, [((group_rows, 2 * half), bf16)], 2, 0, "combine_rows"
    )(returned.reshape(ep_count, back_line), picks)
    return result


def solution(mesh):
    return jax.shard_map(
        on_device,
        mesh=mesh,
        in_specs=(
            P("ep", "etp"),
            P("ep", "etp"),
            P("ep", None),
            P("ep", None),
            P("ep", None, "etp"),
            P("ep", None, "etp"),
            P("ep", "etp", None),
        ),
        out_specs=P("ep", "etp"),
        check_vma=False,
    )
```

```python
import jax
import jax.numpy as jnp
from jax import lax
from jax.experimental import pallas as pl
from jax.experimental.pallas import tpu as pltpu
from jax.sharding import PartitionSpec as P

SIDE = 4
STEPS = (0, 1, 3, 2)
NT = (((1,), (1,)), ((), ()))
NN = (((1,), (0,)), ((), ()))
TN = (((0,), (0,)), ((), ()))
LANES = 128
VMEM_BYTES = 24 * 1024 * 1024


def mm(a, b, dims, precision=None):
    return lax.dot_general(a, b, dims, precision=precision, preferred_element_type=jnp.float32)


def in_vmem(kernel, shapes, count, flops, name):
    return pl.pallas_call(
        kernel,
        out_shape=[jax.ShapeDtypeStruct(*shape) for shape in shapes],
        in_specs=[pl.BlockSpec(memory_space=pltpu.VMEM)] * count,
        out_specs=[pl.BlockSpec(memory_space=pltpu.VMEM)] * len(shapes),
        compiler_params=pltpu.CompilerParams(vmem_limit_bytes=VMEM_BYTES),
        cost_estimate=pl.CostEstimate(flops=flops, bytes_accessed=2_000_000, transcendentals=0),
        name=name,
    )


def pack_kernel(gate_any, up_any, down_any, own, ahead, behind, far_low, far_high, sems):
    quarter = gate_any.shape[0] // SIDE
    lanes = gate_any.shape[1]
    mine = lax.axis_index("etp") // SIDE
    copies = []

    def go(source, target):
        copy = pltpu.make_async_copy(source, target, sems.at[len(copies)])
        copy.start()
        copies.append(copy)

    for step, into in ((2, (far_low, far_high)), (1, (ahead,)), (3, (behind,)), (0, (own,))):
        first = pl.multiple_of(lax.rem(mine + step, SIDE) * quarter, lanes)
        cut = into[0].shape[0] - quarter
        go(gate_any.at[pl.ds(first, quarter)], into[0].at[pl.ds(0, quarter)])
        if len(into) == 1:
            go(up_any.at[pl.ds(first, quarter)], into[0].at[pl.ds(quarter, quarter)])
            base = 2 * quarter
        else:
            go(up_any.at[pl.ds(first, cut)], into[0].at[pl.ds(quarter, cut)])
            go(up_any.at[pl.ds(first + cut, quarter - cut)], into[1].at[pl.ds(0, quarter - cut)])
            base = quarter - cut
        for j in range(quarter // lanes):
            at = pl.multiple_of(first + j * lanes, lanes)
            go(down_any.at[:, pl.ds(at, lanes)], into[-1].at[pl.ds(base + j * lanes, lanes)])
    for copy in copies:
        copy.wait()


def pack_weights(gate, up, down):
    quarter = gate.shape[0] // SIDE
    lanes = gate.shape[1]
    whole = jax.ShapeDtypeStruct((3 * quarter, lanes), gate.dtype)
    part = jax.ShapeDtypeStruct((3 * quarter // 2, lanes), gate.dtype)
    shapes = [whole, whole, whole, part, part]
    return pl.pallas_call(
        pack_kernel,
        out_shape=shapes,
        in_specs=[pl.BlockSpec(memory_space=pl.ANY)] * 3,
        out_specs=[pl.BlockSpec(memory_space=pltpu.VMEM)] * len(shapes),
        scratch_shapes=[pltpu.SemaphoreType.DMA((SIDE * (2 + quarter // lanes) + 1,))],
        compiler_params=pltpu.CompilerParams(vmem_limit_bytes=60 * 1024 * 1024),
        cost_estimate=pl.CostEstimate(flops=0, bytes_accessed=6_000_000, transcendentals=0),
        name="pack_weights",
    )(gate, up, down)


def dispatch_kernel(routes_any, gates_any, tokens_any, grads_any, sent_out, picks_out, *rest):
    routes_ref, gates_ref, tokens_ref, grads_ref, sems = rest
    pairs = (
        (routes_any, routes_ref),
        (gates_any, gates_ref),
        (tokens_any, tokens_ref),
        (grads_any, grads_ref),
    )
    copies = [pltpu.make_async_copy(*pair, sems.at[n]) for n, pair in enumerate(pairs)]
    for copy in copies:
        copy.start()
    for copy in copies:
        copy.wait()
    top, group = routes_ref.shape
    capacity, sides, _ = picks_out.shape
    half = tokens_ref.shape[1] // 2
    expert = lax.broadcasted_iota(jnp.int32, (sides, group), 0) // 2
    member = jnp.zeros((sides, group), jnp.float32)
    weight = jnp.zeros((sides, group), jnp.float32)
    for k in range(top):
        named = expert == routes_ref[k : k + 1, :]
        member = jnp.where(named, 1.0, member)
        weight = jnp.where(named, gates_ref[k : k + 1, :], weight)
    earlier = lax.broadcasted_iota(jnp.int32, (group, group), 0) < lax.broadcasted_iota(
        jnp.int32, (group, group), 1
    )
    rank = mm(member, earlier.astype(jnp.float32), NN)
    even = lax.broadcasted_iota(jnp.int32, (sides, half), 0) % 2 == 0
    tokens = tokens_ref[...].astype(jnp.float32)
    grads = grads_ref[...].astype(jnp.float32)
    input_parts, grad_parts = [], []
    for s in range(capacity):
        pick = jnp.where((rank > s - 0.5) & (rank < s + 0.5), member, 0.0)
        picks_out[s] = pick
        one = mm(pick, tokens, NN)
        two = mm(pick * weight, grads, NN, lax.Precision.HIGHEST)
        input_parts.append(jnp.where(even, one[:, :half], one[:, half:]))
        grad_parts.append(jnp.where(even, two[:, :half], two[:, half:]))
    fill = jnp.zeros((sides, sent_out.shape[2] - capacity * half), jnp.float32)
    sent_out[:, 0, :] = jnp.concatenate([*input_parts, fill], axis=1).astype(sent_out.dtype)
    sent_out[:, 1, :] = jnp.concatenate([*grad_parts, fill], axis=1).astype(sent_out.dtype)


def dispatch_rows(routes, gates, tokens, grads, capacity, sides, line):
    small = (routes, gates, tokens, grads)
    return pl.pallas_call(
        dispatch_kernel,
        out_shape=[
            jax.ShapeDtypeStruct((sides, 2, line), tokens.dtype),
            jax.ShapeDtypeStruct((capacity, sides, routes.shape[1]), jnp.float32),
        ],
        in_specs=[pl.BlockSpec(memory_space=pl.ANY)] * len(small),
        out_specs=[pl.BlockSpec(memory_space=pltpu.VMEM)] * 2,
        scratch_shapes=[
            *[pltpu.VMEM(array.shape, array.dtype) for array in small],
            pltpu.SemaphoreType.DMA((len(small),)),
        ],
        compiler_params=pltpu.CompilerParams(vmem_limit_bytes=60 * 1024 * 1024),
        cost_estimate=pl.CostEstimate(flops=0, bytes_accessed=500_000, transcendentals=0),
        name="dispatch_rows",
    )(*small)


def rows_of(parts, first, count):
    for part in parts:
        if first < part.shape[0]:
            return part[pl.ds(first, count), :]
        first -= part.shape[0]
    return None


def spread_kernel(inputs_ref, grads_ref, out_ref):
    groups = inputs_ref.shape[0]
    half = out_ref.shape[3]
    for which, ref in enumerate((inputs_ref, grads_ref)):
        for s in range(out_ref.shape[2] // groups):
            block = ref[:, s * half : (s + 1) * half]
            for x in range(SIDE):
                out_ref[x, which, pl.ds(s * groups, groups), :] = block


def forward_kernel(x_ref, own, ahead, behind, far_low, far_high, keep_ref, send_ref):
    share = x_ref.shape[3]
    quarter = SIDE * share
    lanes = own.shape[1]
    rows = keep_ref.shape[2]
    mine = lax.axis_index("etp") // SIDE
    core = lax.rem(lax.axis_index("ep"), 2)
    for step, w in zip(STEPS, ((own,), (ahead,), (behind,), (far_low, far_high))):
        place = lax.rem(mine + step, SIDE)
        down = jnp.concatenate(
            [rows_of(w, 2 * quarter + j * lanes, lanes) for j in range(quarter // lanes)], axis=1
        )
        for out_ref, side in ((keep_ref, core), (send_ref, 1 - core)):
            here = pl.ds(pl.multiple_of(side * rows, 32), rows)
            both = None
            hidden = None
            for x in range(SIDE):
                pair = jnp.concatenate(
                    [rows_of(w, x * share, share), rows_of(w, quarter + x * share, share)],
                    axis=1,
                )
                one = mm(x_ref[x, 0, here, :], pair, NN)
                two = mm(x_ref[x, 1, here, :], down[:, x * share : (x + 1) * share], NT)
                both = one if both is None else both + one
                hidden = two if hidden is None else hidden + two
            out_ref[place, 0] = both[:, :lanes].astype(out_ref.dtype)
            out_ref[place, 1] = both[:, lanes:].astype(out_ref.dtype)
            out_ref[place, 2] = hidden.astype(out_ref.dtype)


def backward_kernel(d_ref, own, ahead, behind, far_low, far_high, out_ref):
    share = out_ref.shape[2]
    quarter = SIDE * share
    mine = lax.axis_index("etp") // SIDE
    grads = []
    for step in STEPS:
        place = lax.rem(mine + step, SIDE)
        grads.append(
            jnp.concatenate(
                [
                    jnp.concatenate([d_ref[side, place, 0], d_ref[side, place, 1]], axis=1)
                    for side in range(2)
                ],
                axis=0,
            )
        )
    for x in range(SIDE):
        total = None
        for grad, w in zip(grads, ((own,), (ahead,), (behind,), (far_low, far_high))):
            pair = jnp.concatenate(
                [rows_of(w, x * share, share), rows_of(w, quarter + x * share, share)], axis=1
            )
            one = mm(grad, pair, NT)
            total = one if total is None else total + one
        out_ref[x] = total.astype(out_ref.dtype)


def gather_kernel(parts_ref, out_ref):
    groups = out_ref.shape[0]
    width = out_ref.shape[2]
    half = parts_ref.shape[2]
    capacity = parts_ref.shape[1] // groups
    blocks = []
    for s in range(capacity):
        here = pl.ds(s * groups, groups)
        total = parts_ref[0, here, :].astype(jnp.float32)
        for x in range(1, SIDE):
            total = total + parts_ref[x, here, :].astype(jnp.float32)
        blocks.append(total)
    blocks.append(jnp.zeros((groups, 2 * width - capacity * half), jnp.float32))
    line = jnp.concatenate(blocks, axis=1).astype(out_ref.dtype)
    out_ref[:, 0, :] = line[:, :width]
    out_ref[:, 1, :] = line[:, width:]


def combine_kernel(came_ref, picks_ref, out_ref):
    capacity, sides, group = picks_ref.shape
    half = out_ref.shape[1] // 2
    odd = lax.broadcasted_iota(jnp.int32, (sides, group), 0) % 2
    totals = [None, None]
    for s in range(capacity):
        block = came_ref[:, s * half : (s + 1) * half].astype(jnp.float32)
        for side in range(2):
            one = mm(jnp.where(odd == side, picks_ref[s], 0.0), block, TN)
            totals[side] = one if totals[side] is None else totals[side] + one
    out_ref[...] = jnp.concatenate(totals, axis=1).astype(out_ref.dtype)


def on_device(tokens, grad_out, routes, route_gates, gate_weight, up_weight, down_weight):
    bf16 = jnp.bfloat16
    ep_count = lax.axis_size("ep")
    experts = ep_count // 2
    group_rows, top_count = routes.shape
    capacity = min(group_rows, 5 * group_rows * top_count // (4 * experts))
    half = tokens.shape[1] // 2
    rows_all = ep_count * capacity
    lanes = gate_weight.shape[2]
    quarter = gate_weight.shape[1] // SIDE
    line = -(-capacity * half // LANES) * LANES
    back_line = -(-capacity * half // (2 * LANES)) * 2 * LANES
    along_x = [[SIDE * y + x for x in range(SIDE)] for y in range(SIDE)]
    along_y = [[SIDE * y + x for y in range(SIDE)] for x in range(SIDE)]
    cores = [[2 * z, 2 * z + 1] for z in range(experts)]

    sent, picks = dispatch_rows(
        routes.T, route_gates.T, tokens, grad_out, capacity, ep_count, line
    )
    own, to_ahead, to_behind, to_far_low, to_far_high = pack_weights(
        gate_weight[0], up_weight[0], down_weight[0]
    )

    def shift(block, step):
        pairs = [
            (SIDE * y + x, SIDE * ((y + step) % SIDE) + x) for y in range(SIDE) for x in range(SIDE)
        ]
        return lax.ppermute(block, "etp", pairs)

    weights = [
        own,
        shift(to_behind, -1),
        shift(to_ahead, 1),
        shift(to_far_low, 1),
        shift(to_far_high, -1),
    ]

    came = lax.all_to_all(sent, "ep", split_axis=0, concat_axis=0, tiled=True)
    came, *weights = lax.optimization_barrier((came, *weights))
    weights[3:] = [shift(weights[3], 1), shift(weights[4], -1)]
    (wide,) = in_vmem(
        spread_kernel, [((SIDE, 2, rows_all, half), bf16)], 2, 0, "spread_rows"
    )(came[:, 0], came[:, 1])
    gathered = lax.all_to_all(wide, "etp", 0, 0, tiled=True, axis_index_groups=along_x)

    flops = 2 * 3 * rows_all * quarter * lanes * SIDE
    part = (SIDE, 3, rows_all // 2, lanes)
    keep, send = in_vmem(
        forward_kernel, [(part, jnp.float32), (part, bf16)], 6, flops, "forward_parts"
    )(gathered, *weights)
    other = lax.ppermute(send, "ep", [(i, i ^ 1) for i in range(ep_count)])
    partial = (keep + other.astype(jnp.float32)).astype(bf16)
    partial = lax.all_to_all(partial, "etp", 0, 0, tiled=True, axis_index_groups=along_y)
    pre_gate, pre_up, d_hidden = jnp.sum(partial.astype(jnp.float32), axis=0)
    sigma = jax.nn.sigmoid(pre_gate)
    d_up = (d_hidden * pre_gate * sigma).astype(bf16)
    d_gate = (d_hidden * pre_up * sigma * (1.0 + pre_gate * (1.0 - sigma))).astype(bf16)
    grads = jnp.broadcast_to(jnp.stack([d_gate, d_up])[None], (SIDE, 2, *d_up.shape))
    grads = lax.all_to_all(grads, "etp", 0, 0, tiled=True, axis_index_groups=along_y)
    grads = lax.all_gather(grads, "ep", axis_index_groups=cores)
    (back,) = in_vmem(
        backward_kernel, [((SIDE, rows_all, half), bf16)], 6, flops * 2 // 3, "backward_parts"
    )(grads, *weights)
    back = lax.all_to_all(back, "etp", 0, 0, tiled=True, axis_index_groups=along_x)
    (summed,) = in_vmem(gather_kernel, [((ep_count, 2, back_line // 2), bf16)], 1, 0, "gather_rows")(back)
    returned = lax.all_to_all(summed, "ep", split_axis=0, concat_axis=0, tiled=True)
    (result,) = in_vmem(
        combine_kernel, [((group_rows, 2 * half), bf16)], 2, 0, "combine_rows"
    )(returned.reshape(ep_count, back_line), picks)
    return result


def solution(mesh):
    return jax.shard_map(
        on_device,
        mesh=mesh,
        in_specs=(
            P("ep", "etp"),
            P("ep", "etp"),
            P("ep", None),
            P("ep", None),
            P("ep", None, "etp"),
            P("ep", None, "etp"),
            P("ep", "etp", None),
        ),
        out_specs=P("ep", "etp"),
        check_vma=False,
    )
```

```python
import functools

import jax
import jax.numpy as jnp
from jax import lax
from jax.experimental import pallas as pl
from jax.experimental.pallas import tpu as pltpu
from jax.sharding import PartitionSpec as P

SIDE = 4
STEPS = (0, 1, 3, 2)
NT = (((1,), (1,)), ((), ()))
NN = (((1,), (0,)), ((), ()))
TN = (((0,), (0,)), ((), ()))
LANES = 128
VMEM_BYTES = 24 * 1024 * 1024


def mm(a, b, dims, precision=None):
    return lax.dot_general(a, b, dims, precision=precision, preferred_element_type=jnp.float32)


def in_vmem(kernel, shapes, count, flops, name):
    return pl.pallas_call(
        kernel,
        out_shape=[jax.ShapeDtypeStruct(*shape) for shape in shapes],
        in_specs=[pl.BlockSpec(memory_space=pltpu.VMEM)] * count,
        out_specs=[pl.BlockSpec(memory_space=pltpu.VMEM)] * len(shapes),
        compiler_params=pltpu.CompilerParams(vmem_limit_bytes=VMEM_BYTES),
        cost_estimate=pl.CostEstimate(flops=flops, bytes_accessed=2_000_000, transcendentals=0),
        name=name,
    )


def pack_kernel(gate_any, up_any, down_any, own, ahead, behind, far_low, far_high, sems):
    quarter = gate_any.shape[0] // SIDE
    lanes = gate_any.shape[1]
    mine = lax.axis_index("etp") // SIDE
    copies = []

    def go(source, target):
        copy = pltpu.make_async_copy(source, target, sems.at[len(copies)])
        copy.start()
        copies.append(copy)

    for step, into in ((2, (far_low, far_high)), (1, (ahead,)), (3, (behind,)), (0, (own,))):
        first = pl.multiple_of(lax.rem(mine + step, SIDE) * quarter, lanes)
        cut = into[0].shape[0] - quarter
        go(gate_any.at[pl.ds(first, quarter)], into[0].at[pl.ds(0, quarter)])
        if len(into) == 1:
            go(up_any.at[pl.ds(first, quarter)], into[0].at[pl.ds(quarter, quarter)])
            base = 2 * quarter
        else:
            go(up_any.at[pl.ds(first, cut)], into[0].at[pl.ds(quarter, cut)])
            go(up_any.at[pl.ds(first + cut, quarter - cut)], into[1].at[pl.ds(0, quarter - cut)])
            base = quarter - cut
        for j in range(quarter // lanes):
            at = pl.multiple_of(first + j * lanes, lanes)
            go(down_any.at[:, pl.ds(at, lanes)], into[-1].at[pl.ds(base + j * lanes, lanes)])
    for copy in copies:
        copy.wait()


def pack_weights(gate, up, down):
    quarter = gate.shape[0] // SIDE
    lanes = gate.shape[1]
    whole = jax.ShapeDtypeStruct((3 * quarter, lanes), gate.dtype)
    part = jax.ShapeDtypeStruct((3 * quarter // 2, lanes), gate.dtype)
    shapes = [whole, whole, whole, part, part]
    return pl.pallas_call(
        pack_kernel,
        out_shape=shapes,
        in_specs=[pl.BlockSpec(memory_space=pl.ANY)] * 3,
        out_specs=[pl.BlockSpec(memory_space=pltpu.VMEM)] * len(shapes),
        scratch_shapes=[pltpu.SemaphoreType.DMA((SIDE * (2 + quarter // lanes) + 1,))],
        compiler_params=pltpu.CompilerParams(vmem_limit_bytes=60 * 1024 * 1024),
        cost_estimate=pl.CostEstimate(flops=0, bytes_accessed=6_000_000, transcendentals=0),
        name="pack_weights",
    )(gate, up, down)


def dispatch_kernel(routes_any, gates_any, tokens_any, grads_any, sent_out, picks_out, *rest):
    routes_ref, gates_ref, tokens_ref, grads_ref, sems = rest
    pairs = (
        (routes_any, routes_ref),
        (gates_any, gates_ref),
        (tokens_any, tokens_ref),
        (grads_any, grads_ref),
    )
    copies = [pltpu.make_async_copy(*pair, sems.at[n]) for n, pair in enumerate(pairs)]
    for copy in copies:
        copy.start()
    for copy in copies:
        copy.wait()
    top, group = routes_ref.shape
    capacity, sides, _ = picks_out.shape
    half = tokens_ref.shape[1] // 2
    expert = lax.broadcasted_iota(jnp.int32, (sides, group), 0) // 2
    member = jnp.zeros((sides, group), jnp.float32)
    weight = jnp.zeros((sides, group), jnp.float32)
    for k in range(top):
        named = expert == routes_ref[k : k + 1, :]
        member = jnp.where(named, 1.0, member)
        weight = jnp.where(named, gates_ref[k : k + 1, :], weight)
    earlier = lax.broadcasted_iota(jnp.int32, (group, group), 0) < lax.broadcasted_iota(
        jnp.int32, (group, group), 1
    )
    rank = mm(member, earlier.astype(jnp.float32), NN)
    even = lax.broadcasted_iota(jnp.int32, (sides, half), 0) % 2 == 0
    tokens = tokens_ref[...].astype(jnp.float32)
    grads = grads_ref[...].astype(jnp.float32)
    input_parts, grad_parts = [], []
    for s in range(capacity):
        pick = jnp.where((rank > s - 0.5) & (rank < s + 0.5), member, 0.0)
        picks_out[s] = pick
        one = mm(pick, tokens, NN)
        two = mm(pick * weight, grads, NN, lax.Precision.HIGHEST)
        input_parts.append(jnp.where(even, one[:, :half], one[:, half:]))
        grad_parts.append(jnp.where(even, two[:, :half], two[:, half:]))
    fill = jnp.zeros((sides, sent_out.shape[2] - capacity * half), jnp.float32)
    sent_out[:, 0, :] = jnp.concatenate([*input_parts, fill], axis=1).astype(sent_out.dtype)
    sent_out[:, 1, :] = jnp.concatenate([*grad_parts, fill], axis=1).astype(sent_out.dtype)


def dispatch_rows(routes, gates, tokens, grads, capacity, sides, line):
    small = (routes, gates, tokens, grads)
    return pl.pallas_call(
        dispatch_kernel,
        out_shape=[
            jax.ShapeDtypeStruct((sides, 2, line), tokens.dtype),
            jax.ShapeDtypeStruct((capacity, sides, routes.shape[1]), jnp.float32),
        ],
        in_specs=[pl.BlockSpec(memory_space=pl.ANY)] * len(small),
        out_specs=[pl.BlockSpec(memory_space=pltpu.VMEM)] * 2,
        scratch_shapes=[
            *[pltpu.VMEM(array.shape, array.dtype) for array in small],
            pltpu.SemaphoreType.DMA((len(small),)),
        ],
        compiler_params=pltpu.CompilerParams(vmem_limit_bytes=60 * 1024 * 1024),
        cost_estimate=pl.CostEstimate(flops=0, bytes_accessed=500_000, transcendentals=0),
        name="dispatch_rows",
    )(*small)


def rows_of(parts, first, count):
    for part in parts:
        if first < part.shape[0]:
            return part[pl.ds(first, count), :]
        first -= part.shape[0]
    return None


def forward_kernel(keep, x_ref, own, ahead, behind, far_low, far_high, out_ref):
    quarter = 2 * far_low.shape[0] // 3
    lanes = own.shape[1]
    share = quarter // SIDE
    groups = x_ref.shape[2] // 2
    capacity = out_ref.shape[2] // groups
    mine = lax.axis_index("etp") // SIDE
    core = lax.rem(lax.axis_index("ep"), 2)
    side = core if keep else 1 - core
    here = pl.ds(pl.multiple_of(side * groups, groups), groups)

    def rows(x, which):
        return jnp.concatenate(
            [x_ref[x, which, here, s * share : (s + 1) * share] for s in range(capacity)], axis=0
        )

    inputs = [rows(x, 0) for x in range(SIDE)]
    grads = [rows(x, 1) for x in range(SIDE)]
    for step, w in zip(STEPS, ((own,), (ahead,), (behind,), (far_low, far_high))):
        place = lax.rem(mine + step, SIDE)
        down = jnp.concatenate(
            [rows_of(w, 2 * quarter + j * lanes, lanes) for j in range(quarter // lanes)], axis=1
        )
        both = None
        hidden = None
        for x in range(SIDE):
            pair = jnp.concatenate(
                [rows_of(w, x * share, share), rows_of(w, quarter + x * share, share)],
                axis=1,
            )
            one = mm(inputs[x], pair, NN)
            two = mm(grads[x], down[:, x * share : (x + 1) * share], NT)
            both = one if both is None else both + one
            hidden = two if hidden is None else hidden + two
        out_ref[place, 0] = both[:, :lanes].astype(out_ref.dtype)
        out_ref[place, 1] = both[:, lanes:].astype(out_ref.dtype)
        out_ref[place, 2] = hidden.astype(out_ref.dtype)


def backward_kernel(d_ref, own, ahead, behind, far_low, far_high, out_ref):
    quarter = 2 * far_low.shape[0] // 3
    share = quarter // SIDE
    groups = out_ref.shape[1] // 2
    rows = d_ref.shape[3]
    mine = lax.axis_index("etp") // SIDE
    grads = []
    for step in STEPS:
        place = lax.rem(mine + step, SIDE)
        grads.append(
            jnp.concatenate(
                [
                    jnp.concatenate([d_ref[side, place, 0], d_ref[side, place, 1]], axis=1)
                    for side in range(2)
                ],
                axis=0,
            )
        )
    fill = jnp.zeros((groups, out_ref.shape[2] - rows // groups * share), jnp.float32)
    for x in range(SIDE):
        total = None
        for grad, w in zip(grads, ((own,), (ahead,), (behind,), (far_low, far_high))):
            pair = jnp.concatenate(
                [rows_of(w, x * share, share), rows_of(w, quarter + x * share, share)], axis=1
            )
            one = mm(grad, pair, NT)
            total = one if total is None else total + one
        for side in range(2):
            blocks = [
                total[side * rows + s * groups : side * rows + (s + 1) * groups]
                for s in range(rows // groups)
            ]
            line = jnp.concatenate([*blocks, fill], axis=1)
            out_ref[x, pl.ds(side * groups, groups), :] = line.astype(out_ref.dtype)


def gather_kernel(parts_ref, out_ref):
    width = out_ref.shape[2]
    total = parts_ref[0].astype(jnp.float32)
    for x in range(1, SIDE):
        total = total + parts_ref[x].astype(jnp.float32)
    fill = jnp.zeros((total.shape[0], 2 * width - total.shape[1]), jnp.float32)
    line = jnp.concatenate([total, fill], axis=1).astype(out_ref.dtype)
    out_ref[:, 0, :] = line[:, :width]
    out_ref[:, 1, :] = line[:, width:]


def combine_kernel(came_ref, picks_ref, out_ref):
    capacity, sides, group = picks_ref.shape
    half = out_ref.shape[1] // 2
    odd = lax.broadcasted_iota(jnp.int32, (sides, group), 0) % 2
    totals = [None, None]
    for s in range(capacity):
        block = came_ref[:, s * half : (s + 1) * half].astype(jnp.float32)
        for side in range(2):
            one = mm(jnp.where(odd == side, picks_ref[s], 0.0), block, TN)
            totals[side] = one if totals[side] is None else totals[side] + one
    out_ref[...] = jnp.concatenate(totals, axis=1).astype(out_ref.dtype)


def on_device(tokens, grad_out, routes, route_gates, gate_weight, up_weight, down_weight):
    bf16 = jnp.bfloat16
    ep_count = lax.axis_size("ep")
    experts = ep_count // 2
    group_rows, top_count = routes.shape
    capacity = min(group_rows, 5 * group_rows * top_count // (4 * experts))
    half = tokens.shape[1] // 2
    rows_all = ep_count * capacity
    lanes = gate_weight.shape[2]
    quarter = gate_weight.shape[1] // SIDE
    line = -(-capacity * half // LANES) * LANES
    back_line = -(-capacity * half // (2 * LANES)) * 2 * LANES
    along_x = [[SIDE * y + x for x in range(SIDE)] for y in range(SIDE)]
    along_y = [[SIDE * y + x for y in range(SIDE)] for x in range(SIDE)]
    cores = [[2 * z, 2 * z + 1] for z in range(experts)]

    sent, picks = dispatch_rows(
        routes.T, route_gates.T, tokens, grad_out, capacity, ep_count, line
    )
    own, to_ahead, to_behind, to_far_low, to_far_high = pack_weights(
        gate_weight[0], up_weight[0], down_weight[0]
    )

    def shift(block, step):
        pairs = [
            (SIDE * y + x, SIDE * ((y + step) % SIDE) + x) for y in range(SIDE) for x in range(SIDE)
        ]
        return lax.ppermute(block, "etp", pairs)

    weights = [
        own,
        shift(to_behind, -1),
        shift(to_ahead, 1),
        shift(shift(to_far_low, 1), 1),
        shift(shift(to_far_high, -1), -1),
    ]

    came = lax.all_to_all(sent, "ep", split_axis=0, concat_axis=0, tiled=True)
    came, *weights = lax.optimization_barrier((came, *weights))
    wide = jnp.broadcast_to(came[None], (SIDE, *came.shape))
    gathered = lax.all_to_all(wide, "etp", 0, 0, tiled=True, axis_index_groups=along_x)
    gathered = jnp.swapaxes(gathered, 1, 2)

    flops = 2 * 3 * rows_all * quarter * lanes * SIDE
    part = (SIDE, 3, rows_all // 2, lanes)
    (send,) = in_vmem(
        functools.partial(forward_kernel, False), [(part, bf16)], 6, flops // 2, "forward_send"
    )(gathered, *weights)
    other = lax.ppermute(send, "ep", [(i, i ^ 1) for i in range(ep_count)])
    (keep,) = in_vmem(
        functools.partial(forward_kernel, True), [(part, jnp.float32)], 6, flops // 2, "forward_keep"
    )(gathered, *weights)
    partial = (keep + other.astype(jnp.float32)).astype(bf16)
    partial = lax.all_to_all(partial, "etp", 0, 0, tiled=True, axis_index_groups=along_y)
    pre_gate, pre_up, d_hidden = jnp.sum(partial.astype(jnp.float32), axis=0)
    sigma = jax.nn.sigmoid(pre_gate)
    d_up = (d_hidden * pre_gate * sigma).astype(bf16)
    d_gate = (d_hidden * pre_up * sigma * (1.0 + pre_gate * (1.0 - sigma))).astype(bf16)
    grads = jnp.broadcast_to(jnp.stack([d_gate, d_up])[None], (SIDE, 2, *d_up.shape))
    grads = lax.all_to_all(grads, "etp", 0, 0, tiled=True, axis_index_groups=along_y)
    grads = lax.all_gather(grads, "ep", axis_index_groups=cores)
    (back,) = in_vmem(
        backward_kernel, [((SIDE, ep_count, line), bf16)], 6, flops * 2 // 3, "backward_parts"
    )(grads, *weights)
    back = lax.all_to_all(back, "etp", 0, 0, tiled=True, axis_index_groups=along_x)
    (summed,) = in_vmem(gather_kernel, [((ep_count, 2, back_line // 2), bf16)], 1, 0, "gather_rows")(back)
    returned = lax.all_to_all(summed, "ep", split_axis=0, concat_axis=0, tiled=True)
    (result,) = in_vmem(
        combine_kernel, [((group_rows, 2 * half), bf16)], 2, 0, "combine_rows"
    )(returned.reshape(ep_count, back_line), picks)
    return result


def solution(mesh):
    return jax.shard_map(
        on_device,
        mesh=mesh,
        in_specs=(
            P("ep", "etp"),
            P("ep", "etp"),
            P("ep", None),
            P("ep", None),
            P("ep", None, "etp"),
            P("ep", None, "etp"),
            P("ep", "etp", None),
        ),
        out_specs=P("ep", "etp"),
        check_vma=False,
    )
```

```python
import functools

import jax
import jax.numpy as jnp
from jax import lax
from jax.experimental import pallas as pl
from jax.experimental.pallas import tpu as pltpu
from jax.sharding import PartitionSpec as P

SIDE = 4
STEPS = (0, 1, 3, 2)
NT = (((1,), (1,)), ((), ()))
NN = (((1,), (0,)), ((), ()))
TN = (((0,), (0,)), ((), ()))
LANES = 128
VMEM_BYTES = 24 * 1024 * 1024


def mm(a, b, dims, precision=None):
    return lax.dot_general(a, b, dims, precision=precision, preferred_element_type=jnp.float32)


def in_vmem(kernel, shapes, count, flops, name):
    return pl.pallas_call(
        kernel,
        out_shape=[jax.ShapeDtypeStruct(*shape) for shape in shapes],
        in_specs=[pl.BlockSpec(memory_space=pltpu.VMEM)] * count,
        out_specs=[pl.BlockSpec(memory_space=pltpu.VMEM)] * len(shapes),
        compiler_params=pltpu.CompilerParams(vmem_limit_bytes=VMEM_BYTES),
        cost_estimate=pl.CostEstimate(flops=flops, bytes_accessed=2_000_000, transcendentals=0),
        name=name,
    )


def pack_kernel(steps, gate_any, up_any, down_any, *rest):
    outs, sems = list(rest[:-1]), rest[-1]
    quarter = gate_any.shape[0] // SIDE
    lanes = gate_any.shape[1]
    mine = lax.axis_index("etp") // SIDE
    copies = []

    def go(source, target):
        copy = pltpu.make_async_copy(source, target, sems.at[len(copies)])
        copy.start()
        copies.append(copy)

    for step in steps:
        into = [outs.pop(0)]
        first = pl.multiple_of(lax.rem(mine + step, SIDE) * quarter, lanes)
        cut = into[0].shape[0] - quarter
        go(gate_any.at[pl.ds(first, quarter)], into[0].at[pl.ds(0, quarter)])
        if cut == 2 * quarter:
            go(up_any.at[pl.ds(first, quarter)], into[0].at[pl.ds(quarter, quarter)])
            base = 2 * quarter
        else:
            into.append(outs.pop(0))
            go(up_any.at[pl.ds(first, cut)], into[0].at[pl.ds(quarter, cut)])
            go(up_any.at[pl.ds(first + cut, quarter - cut)], into[1].at[pl.ds(0, quarter - cut)])
            base = quarter - cut
        for j in range(quarter // lanes):
            at = pl.multiple_of(first + j * lanes, lanes)
            go(down_any.at[:, pl.ds(at, lanes)], into[-1].at[pl.ds(base + j * lanes, lanes)])
    for copy in copies:
        copy.wait()


def pack_weights(steps, sizes, gate, up, down):
    lanes = gate.shape[1]
    count = len(steps) * (2 + gate.shape[0] // SIDE // lanes) + len(sizes) - len(steps)
    return pl.pallas_call(
        functools.partial(pack_kernel, steps),
        out_shape=[jax.ShapeDtypeStruct((size, lanes), gate.dtype) for size in sizes],
        in_specs=[pl.BlockSpec(memory_space=pl.ANY)] * 3,
        out_specs=[pl.BlockSpec(memory_space=pltpu.VMEM)] * len(sizes),
        scratch_shapes=[pltpu.SemaphoreType.DMA((count,))],
        compiler_params=pltpu.CompilerParams(vmem_limit_bytes=60 * 1024 * 1024),
        cost_estimate=pl.CostEstimate(flops=0, bytes_accessed=3_000_000, transcendentals=0),
        name="pack_far" if len(sizes) > len(steps) else "pack_near",
    )(gate, up, down)


def dispatch_kernel(routes_any, gates_any, tokens_any, grads_any, sent_out, picks_out, *rest):
    routes_ref, gates_ref, tokens_ref, grads_ref, sems = rest
    pairs = (
        (routes_any, routes_ref),
        (gates_any, gates_ref),
        (tokens_any, tokens_ref),
        (grads_any, grads_ref),
    )
    copies = [pltpu.make_async_copy(*pair, sems.at[n]) for n, pair in enumerate(pairs)]
    for copy in copies:
        copy.start()
    for copy in copies:
        copy.wait()
    top, group = routes_ref.shape
    capacity, sides, _ = picks_out.shape
    half = tokens_ref.shape[1] // 2
    expert = lax.broadcasted_iota(jnp.int32, (sides, group), 0) // 2
    member = jnp.zeros((sides, group), jnp.float32)
    weight = jnp.zeros((sides, group), jnp.float32)
    for k in range(top):
        named = expert == routes_ref[k : k + 1, :]
        member = jnp.where(named, 1.0, member)
        weight = jnp.where(named, gates_ref[k : k + 1, :], weight)
    earlier = lax.broadcasted_iota(jnp.int32, (group, group), 0) < lax.broadcasted_iota(
        jnp.int32, (group, group), 1
    )
    rank = mm(member, earlier.astype(jnp.float32), NN)
    even = lax.broadcasted_iota(jnp.int32, (sides, half), 0) % 2 == 0
    tokens = tokens_ref[...].astype(jnp.float32)
    grads = grads_ref[...].astype(jnp.float32)
    input_parts, grad_parts = [], []
    for s in range(capacity):
        pick = jnp.where((rank > s - 0.5) & (rank < s + 0.5), member, 0.0)
        picks_out[s] = pick
        one = mm(pick, tokens, NN)
        two = mm(pick * weight, grads, NN, lax.Precision.HIGHEST)
        input_parts.append(jnp.where(even, one[:, :half], one[:, half:]))
        grad_parts.append(jnp.where(even, two[:, :half], two[:, half:]))
    fill = jnp.zeros((sides, sent_out.shape[2] - capacity * half), jnp.float32)
    sent_out[:, 0, :] = jnp.concatenate([*input_parts, fill], axis=1).astype(sent_out.dtype)
    sent_out[:, 1, :] = jnp.concatenate([*grad_parts, fill], axis=1).astype(sent_out.dtype)


def dispatch_rows(routes, gates, tokens, grads, capacity, sides, line):
    small = (routes, gates, tokens, grads)
    return pl.pallas_call(
        dispatch_kernel,
        out_shape=[
            jax.ShapeDtypeStruct((sides, 2, line), tokens.dtype),
            jax.ShapeDtypeStruct((capacity, sides, routes.shape[1]), jnp.float32),
        ],
        in_specs=[pl.BlockSpec(memory_space=pl.ANY)] * len(small),
        out_specs=[pl.BlockSpec(memory_space=pltpu.VMEM)] * 2,
        scratch_shapes=[
            *[pltpu.VMEM(array.shape, array.dtype) for array in small],
            pltpu.SemaphoreType.DMA((len(small),)),
        ],
        compiler_params=pltpu.CompilerParams(vmem_limit_bytes=60 * 1024 * 1024),
        cost_estimate=pl.CostEstimate(flops=0, bytes_accessed=500_000, transcendentals=0),
        name="dispatch_rows",
    )(*small)


def rows_of(parts, first, count):
    for part in parts:
        if first < part.shape[0]:
            return part[pl.ds(first, count), :]
        first -= part.shape[0]
    return None


def forward_kernel(keep, x_ref, own, ahead, behind, far_low, far_high, out_ref):
    quarter = own.shape[0] // 3
    lanes = own.shape[1]
    share = quarter // SIDE
    groups = x_ref.shape[2] // 2
    capacity = out_ref.shape[2] // groups
    mine = lax.axis_index("etp") // SIDE
    core = lax.rem(lax.axis_index("ep"), 2)
    side = core if keep else 1 - core
    here = pl.ds(pl.multiple_of(side * groups, groups), groups)

    def rows(x, which):
        return jnp.concatenate(
            [x_ref[x, which, here, s * share : (s + 1) * share] for s in range(capacity)], axis=0
        )

    inputs = [rows(x, 0) for x in range(SIDE)]
    grads = [rows(x, 1) for x in range(SIDE)]
    for step, w in zip(STEPS, ((own,), (ahead,), (behind,), (far_low, far_high))):
        place = lax.rem(mine + step, SIDE)
        down = jnp.concatenate(
            [rows_of(w, 2 * quarter + j * lanes, lanes) for j in range(quarter // lanes)], axis=1
        )
        both = None
        hidden = None
        for x in range(SIDE):
            pair = jnp.concatenate(
                [rows_of(w, x * share, share), rows_of(w, quarter + x * share, share)],
                axis=1,
            )
            one = mm(inputs[x], pair, NN)
            two = mm(grads[x], down[:, x * share : (x + 1) * share], NT)
            both = one if both is None else both + one
            hidden = two if hidden is None else hidden + two
        out_ref[place, 0] = both[:, :lanes].astype(out_ref.dtype)
        out_ref[place, 1] = both[:, lanes:].astype(out_ref.dtype)
        out_ref[place, 2] = hidden.astype(out_ref.dtype)


def backward_kernel(d_ref, own, ahead, behind, far_low, far_high, out_ref):
    quarter = own.shape[0] // 3
    share = quarter // SIDE
    groups = out_ref.shape[1] // 2
    rows = d_ref.shape[3]
    mine = lax.axis_index("etp") // SIDE
    grads = []
    for step in STEPS:
        place = lax.rem(mine + step, SIDE)
        grads.append(
            jnp.concatenate(
                [
                    jnp.concatenate([d_ref[side, place, 0], d_ref[side, place, 1]], axis=1)
                    for side in range(2)
                ],
                axis=0,
            )
        )
    fill = jnp.zeros((groups, out_ref.shape[2] - rows // groups * share), jnp.float32)
    for x in range(SIDE):
        total = None
        for grad, w in zip(grads, ((own,), (ahead,), (behind,), (far_low, far_high))):
            pair = jnp.concatenate(
                [rows_of(w, x * share, share), rows_of(w, quarter + x * share, share)], axis=1
            )
            one = mm(grad, pair, NT)
            total = one if total is None else total + one
        for side in range(2):
            blocks = [
                total[side * rows + s * groups : side * rows + (s + 1) * groups]
                for s in range(rows // groups)
            ]
            line = jnp.concatenate([*blocks, fill], axis=1)
            out_ref[x, pl.ds(side * groups, groups), :] = line.astype(out_ref.dtype)


def gather_kernel(parts_ref, out_ref):
    width = out_ref.shape[2]
    total = parts_ref[0].astype(jnp.float32)
    for x in range(1, SIDE):
        total = total + parts_ref[x].astype(jnp.float32)
    fill = jnp.zeros((total.shape[0], 2 * width - total.shape[1]), jnp.float32)
    line = jnp.concatenate([total, fill], axis=1).astype(out_ref.dtype)
    out_ref[:, 0, :] = line[:, :width]
    out_ref[:, 1, :] = line[:, width:]


def combine_kernel(came_ref, picks_ref, out_ref):
    capacity, sides, group = picks_ref.shape
    half = out_ref.shape[1] // 2
    odd = lax.broadcasted_iota(jnp.int32, (sides, group), 0) % 2
    totals = [None, None]
    for s in range(capacity):
        block = came_ref[:, s * half : (s + 1) * half].astype(jnp.float32)
        for side in range(2):
            one = mm(jnp.where(odd == side, picks_ref[s], 0.0), block, TN)
            totals[side] = one if totals[side] is None else totals[side] + one
    out_ref[...] = jnp.concatenate(totals, axis=1).astype(out_ref.dtype)


def on_device(tokens, grad_out, routes, route_gates, gate_weight, up_weight, down_weight):
    bf16 = jnp.bfloat16
    ep_count = lax.axis_size("ep")
    experts = ep_count // 2
    group_rows, top_count = routes.shape
    capacity = min(group_rows, 5 * group_rows * top_count // (4 * experts))
    half = tokens.shape[1] // 2
    rows_all = ep_count * capacity
    lanes = gate_weight.shape[2]
    quarter = gate_weight.shape[1] // SIDE
    line = -(-capacity * half // LANES) * LANES
    back_line = -(-capacity * half // (2 * LANES)) * 2 * LANES
    along_x = [[SIDE * y + x for x in range(SIDE)] for y in range(SIDE)]
    along_y = [[SIDE * y + x for y in range(SIDE)] for x in range(SIDE)]
    cores = [[2 * z, 2 * z + 1] for z in range(experts)]

    sent, picks = dispatch_rows(
        routes.T, route_gates.T, tokens, grad_out, capacity, ep_count, line
    )
    ours = (gate_weight[0], up_weight[0], down_weight[0])
    low = quarter + quarter // 2
    to_far_low, to_far_high = pack_weights((2,), (low, 3 * quarter - low), *ours)
    to_ahead, to_behind, own = pack_weights((1, 3, 0), (3 * quarter,) * 3, *ours)

    def shift(block, step):
        pairs = [
            (SIDE * y + x, SIDE * ((y + step) % SIDE) + x) for y in range(SIDE) for x in range(SIDE)
        ]
        return lax.ppermute(block, "etp", pairs)

    weights = [
        own,
        shift(to_behind, -1),
        shift(to_ahead, 1),
        shift(shift(to_far_low, 1), 1),
        shift(shift(to_far_high, -1), -1),
    ]

    came = lax.all_to_all(sent, "ep", split_axis=0, concat_axis=0, tiled=True)
    came, *weights = lax.optimization_barrier((came, *weights))
    wide = jnp.broadcast_to(came[None], (SIDE, *came.shape))
    gathered = lax.all_to_all(wide, "etp", 0, 0, tiled=True, axis_index_groups=along_x)
    gathered = jnp.swapaxes(gathered, 1, 2)

    flops = 2 * 3 * rows_all * quarter * lanes * SIDE
    part = (SIDE, 3, rows_all // 2, lanes)
    (send,) = in_vmem(
        functools.partial(forward_kernel, False), [(part, bf16)], 6, flops // 2, "forward_send"
    )(gathered, *weights)
    other = lax.ppermute(send, "ep", [(i, i ^ 1) for i in range(ep_count)])
    (keep,) = in_vmem(
        functools.partial(forward_kernel, True), [(part, jnp.float32)], 6, flops // 2, "forward_keep"
    )(gathered, *weights)
    partial = (keep + other.astype(jnp.float32)).astype(bf16)
    partial = lax.all_to_all(partial, "etp", 0, 0, tiled=True, axis_index_groups=along_y)
    pre_gate, pre_up, d_hidden = jnp.sum(partial.astype(jnp.float32), axis=0)
    sigma = jax.nn.sigmoid(pre_gate)
    d_up = (d_hidden * pre_gate * sigma).astype(bf16)
    d_gate = (d_hidden * pre_up * sigma * (1.0 + pre_gate * (1.0 - sigma))).astype(bf16)
    grads = jnp.broadcast_to(jnp.stack([d_gate, d_up])[None], (SIDE, 2, *d_up.shape))
    grads = lax.all_to_all(grads, "etp", 0, 0, tiled=True, axis_index_groups=along_y)
    grads = lax.all_gather(grads, "ep", axis_index_groups=cores)
    (back,) = in_vmem(
        backward_kernel, [((SIDE, ep_count, line), bf16)], 6, flops * 2 // 3, "backward_parts"
    )(grads, *weights)
    back = lax.all_to_all(back, "etp", 0, 0, tiled=True, axis_index_groups=along_x)
    (summed,) = in_vmem(gather_kernel, [((ep_count, 2, back_line // 2), bf16)], 1, 0, "gather_rows")(back)
    returned = lax.all_to_all(summed, "ep", split_axis=0, concat_axis=0, tiled=True)
    (result,) = in_vmem(
        combine_kernel, [((group_rows, 2 * half), bf16)], 2, 0, "combine_rows"
    )(returned.reshape(ep_count, back_line), picks)
    return result


def solution(mesh):
    return jax.shard_map(
        on_device,
        mesh=mesh,
        in_specs=(
            P("ep", "etp"),
            P("ep", "etp"),
            P("ep", None),
            P("ep", None),
            P("ep", None, "etp"),
            P("ep", None, "etp"),
            P("ep", "etp", None),
        ),
        out_specs=P("ep", "etp"),
        check_vma=False,
    )
```

```python
import functools

import jax
import jax.numpy as jnp
from jax import lax
from jax.experimental import pallas as pl
from jax.experimental.pallas import tpu as pltpu
from jax.sharding import PartitionSpec as P

SIDE = 4
STEPS = (0, 1, 3, 2)
NT = (((1,), (1,)), ((), ()))
NN = (((1,), (0,)), ((), ()))
TN = (((0,), (0,)), ((), ()))
LANES = 128
VMEM_BYTES = 24 * 1024 * 1024


def mm(a, b, dims, precision=None):
    return lax.dot_general(a, b, dims, precision=precision, preferred_element_type=jnp.float32)


def in_vmem(kernel, shapes, count, flops, name):
    return pl.pallas_call(
        kernel,
        out_shape=[jax.ShapeDtypeStruct(*shape) for shape in shapes],
        in_specs=[pl.BlockSpec(memory_space=pltpu.VMEM)] * count,
        out_specs=[pl.BlockSpec(memory_space=pltpu.VMEM)] * len(shapes),
        compiler_params=pltpu.CompilerParams(vmem_limit_bytes=VMEM_BYTES),
        cost_estimate=pl.CostEstimate(flops=flops, bytes_accessed=2_000_000, transcendentals=0),
        name=name,
    )


def pack_kernel(steps, gate_any, up_any, down_any, *rest):
    outs, sems = list(rest[:-1]), rest[-1]
    quarter = gate_any.shape[0] // SIDE
    lanes = gate_any.shape[1]
    mine = lax.axis_index("etp") // SIDE
    copies = []

    def go(source, target):
        copy = pltpu.make_async_copy(source, target, sems.at[len(copies)])
        copy.start()
        copies.append(copy)

    for step in steps:
        into = [outs.pop(0)]
        first = pl.multiple_of(lax.rem(mine + step, SIDE) * quarter, lanes)
        cut = into[0].shape[0] - quarter
        go(gate_any.at[pl.ds(first, quarter)], into[0].at[pl.ds(0, quarter)])
        if cut == 2 * quarter:
            go(up_any.at[pl.ds(first, quarter)], into[0].at[pl.ds(quarter, quarter)])
            base = 2 * quarter
        else:
            into.append(outs.pop(0))
            go(up_any.at[pl.ds(first, cut)], into[0].at[pl.ds(quarter, cut)])
            go(up_any.at[pl.ds(first + cut, quarter - cut)], into[1].at[pl.ds(0, quarter - cut)])
            base = quarter - cut
        for j in range(quarter // lanes):
            at = pl.multiple_of(first + j * lanes, lanes)
            go(down_any.at[:, pl.ds(at, lanes)], into[-1].at[pl.ds(base + j * lanes, lanes)])
    for copy in copies:
        copy.wait()


def pack_weights(steps, sizes, gate, up, down):
    lanes = gate.shape[1]
    count = len(steps) * (2 + gate.shape[0] // SIDE // lanes) + len(sizes) - len(steps)
    return pl.pallas_call(
        functools.partial(pack_kernel, steps),
        out_shape=[jax.ShapeDtypeStruct((size, lanes), gate.dtype) for size in sizes],
        in_specs=[pl.BlockSpec(memory_space=pl.ANY)] * 3,
        out_specs=[pl.BlockSpec(memory_space=pltpu.VMEM)] * len(sizes),
        scratch_shapes=[pltpu.SemaphoreType.DMA((count,))],
        compiler_params=pltpu.CompilerParams(vmem_limit_bytes=60 * 1024 * 1024),
        cost_estimate=pl.CostEstimate(flops=0, bytes_accessed=3_000_000, transcendentals=0),
        name=f"pack_{steps[0]}",
    )(gate, up, down)


def dispatch_kernel(routes_any, gates_any, tokens_any, grads_any, sent_out, picks_out, *rest):
    routes_ref, gates_ref, tokens_ref, grads_ref, sems = rest
    pairs = (
        (routes_any, routes_ref),
        (gates_any, gates_ref),
        (tokens_any, tokens_ref),
        (grads_any, grads_ref),
    )
    copies = [pltpu.make_async_copy(*pair, sems.at[n]) for n, pair in enumerate(pairs)]
    for copy in copies:
        copy.start()
    for copy in copies:
        copy.wait()
    top, group = routes_ref.shape
    capacity, sides, _ = picks_out.shape
    half = tokens_ref.shape[1] // 2
    expert = lax.broadcasted_iota(jnp.int32, (sides, group), 0) // 2
    member = jnp.zeros((sides, group), jnp.float32)
    weight = jnp.zeros((sides, group), jnp.float32)
    for k in range(top):
        named = expert == routes_ref[k : k + 1, :]
        member = jnp.where(named, 1.0, member)
        weight = jnp.where(named, gates_ref[k : k + 1, :], weight)
    earlier = lax.broadcasted_iota(jnp.int32, (group, group), 0) < lax.broadcasted_iota(
        jnp.int32, (group, group), 1
    )
    rank = mm(member, earlier.astype(jnp.float32), NN)
    even = lax.broadcasted_iota(jnp.int32, (sides, half), 0) % 2 == 0
    tokens = tokens_ref[...].astype(jnp.float32)
    grads = grads_ref[...].astype(jnp.float32)
    input_parts, grad_parts = [], []
    for s in range(capacity):
        pick = jnp.where((rank > s - 0.5) & (rank < s + 0.5), member, 0.0)
        picks_out[s] = pick
        one = mm(pick, tokens, NN)
        two = mm(pick * weight, grads, NN, lax.Precision.HIGHEST)
        input_parts.append(jnp.where(even, one[:, :half], one[:, half:]))
        grad_parts.append(jnp.where(even, two[:, :half], two[:, half:]))
    fill = jnp.zeros((sides, sent_out.shape[2] - capacity * half), jnp.float32)
    sent_out[:, 0, :] = jnp.concatenate([*input_parts, fill], axis=1).astype(sent_out.dtype)
    sent_out[:, 1, :] = jnp.concatenate([*grad_parts, fill], axis=1).astype(sent_out.dtype)


def dispatch_rows(routes, gates, tokens, grads, capacity, sides, line):
    small = (routes, gates, tokens, grads)
    return pl.pallas_call(
        dispatch_kernel,
        out_shape=[
            jax.ShapeDtypeStruct((sides, 2, line), tokens.dtype),
            jax.ShapeDtypeStruct((capacity, sides, routes.shape[1]), jnp.float32),
        ],
        in_specs=[pl.BlockSpec(memory_space=pl.ANY)] * len(small),
        out_specs=[pl.BlockSpec(memory_space=pltpu.VMEM)] * 2,
        scratch_shapes=[
            *[pltpu.VMEM(array.shape, array.dtype) for array in small],
            pltpu.SemaphoreType.DMA((len(small),)),
        ],
        compiler_params=pltpu.CompilerParams(vmem_limit_bytes=60 * 1024 * 1024),
        cost_estimate=pl.CostEstimate(flops=0, bytes_accessed=500_000, transcendentals=0),
        name="dispatch_rows",
    )(*small)


def rows_of(parts, first, count):
    for part in parts:
        if first < part.shape[0]:
            return part[pl.ds(first, count), :]
        first -= part.shape[0]
    return None


def forward_kernel(keep, x_ref, own, ahead, behind, far_low, far_high, out_ref):
    quarter = own.shape[0] // 3
    lanes = own.shape[1]
    share = quarter // SIDE
    groups = x_ref.shape[2] // 2
    capacity = out_ref.shape[2] // groups
    mine = lax.axis_index("etp") // SIDE
    core = lax.rem(lax.axis_index("ep"), 2)
    side = core if keep else 1 - core
    here = pl.ds(pl.multiple_of(side * groups, groups), groups)

    def rows(x, which):
        return jnp.concatenate(
            [x_ref[x, which, here, s * share : (s + 1) * share] for s in range(capacity)], axis=0
        )

    inputs = [rows(x, 0) for x in range(SIDE)]
    grads = [rows(x, 1) for x in range(SIDE)]
    for step, w in zip(STEPS, ((own,), (ahead,), (behind,), (far_low, far_high))):
        place = lax.rem(mine + step, SIDE)
        down = jnp.concatenate(
            [rows_of(w, 2 * quarter + j * lanes, lanes) for j in range(quarter // lanes)], axis=1
        )
        both = None
        hidden = None
        for x in range(SIDE):
            pair = jnp.concatenate(
                [rows_of(w, x * share, share), rows_of(w, quarter + x * share, share)],
                axis=1,
            )
            one = mm(inputs[x], pair, NN)
            two = mm(grads[x], down[:, x * share : (x + 1) * share], NT)
            both = one if both is None else both + one
            hidden = two if hidden is None else hidden + two
        out_ref[place, 0] = both[:, :lanes].astype(out_ref.dtype)
        out_ref[place, 1] = both[:, lanes:].astype(out_ref.dtype)
        out_ref[place, 2] = hidden.astype(out_ref.dtype)


def backward_kernel(d_ref, own, ahead, behind, far_low, far_high, out_ref):
    quarter = own.shape[0] // 3
    share = quarter // SIDE
    groups = out_ref.shape[1] // 2
    rows = d_ref.shape[3]
    mine = lax.axis_index("etp") // SIDE
    grads = []
    for step in STEPS:
        place = lax.rem(mine + step, SIDE)
        grads.append(
            jnp.concatenate(
                [
                    jnp.concatenate([d_ref[side, place, 0], d_ref[side, place, 1]], axis=1)
                    for side in range(2)
                ],
                axis=0,
            )
        )
    fill = jnp.zeros((groups, out_ref.shape[2] - rows // groups * share), jnp.float32)
    for x in range(SIDE):
        total = None
        for grad, w in zip(grads, ((own,), (ahead,), (behind,), (far_low, far_high))):
            pair = jnp.concatenate(
                [rows_of(w, x * share, share), rows_of(w, quarter + x * share, share)], axis=1
            )
            one = mm(grad, pair, NT)
            total = one if total is None else total + one
        for side in range(2):
            blocks = [
                total[side * rows + s * groups : side * rows + (s + 1) * groups]
                for s in range(rows // groups)
            ]
            line = jnp.concatenate([*blocks, fill], axis=1)
            out_ref[x, pl.ds(side * groups, groups), :] = line.astype(out_ref.dtype)


def gather_kernel(parts_ref, out_ref):
    width = out_ref.shape[2]
    total = parts_ref[0].astype(jnp.float32)
    for x in range(1, SIDE):
        total = total + parts_ref[x].astype(jnp.float32)
    fill = jnp.zeros((total.shape[0], 2 * width - total.shape[1]), jnp.float32)
    line = jnp.concatenate([total, fill], axis=1).astype(out_ref.dtype)
    out_ref[:, 0, :] = line[:, :width]
    out_ref[:, 1, :] = line[:, width:]


def combine_kernel(came_ref, picks_ref, out_ref):
    capacity, sides, group = picks_ref.shape
    half = out_ref.shape[1] // 2
    odd = lax.broadcasted_iota(jnp.int32, (sides, group), 0) % 2
    totals = [None, None]
    for s in range(capacity):
        block = came_ref[:, s * half : (s + 1) * half].astype(jnp.float32)
        for side in range(2):
            one = mm(jnp.where(odd == side, picks_ref[s], 0.0), block, TN)
            totals[side] = one if totals[side] is None else totals[side] + one
    out_ref[...] = jnp.concatenate(totals, axis=1).astype(out_ref.dtype)


def on_device(tokens, grad_out, routes, route_gates, gate_weight, up_weight, down_weight):
    bf16 = jnp.bfloat16
    ep_count = lax.axis_size("ep")
    experts = ep_count // 2
    group_rows, top_count = routes.shape
    capacity = min(group_rows, 5 * group_rows * top_count // (4 * experts))
    half = tokens.shape[1] // 2
    rows_all = ep_count * capacity
    lanes = gate_weight.shape[2]
    quarter = gate_weight.shape[1] // SIDE
    line = -(-capacity * half // LANES) * LANES
    back_line = -(-capacity * half // (2 * LANES)) * 2 * LANES
    along_x = [[SIDE * y + x for x in range(SIDE)] for y in range(SIDE)]
    along_y = [[SIDE * y + x for y in range(SIDE)] for x in range(SIDE)]
    cores = [[2 * z, 2 * z + 1] for z in range(experts)]

    sent, picks = dispatch_rows(
        routes.T, route_gates.T, tokens, grad_out, capacity, ep_count, line
    )
    ours = (gate_weight[0], up_weight[0], down_weight[0])
    low = quarter + quarter // 2
    to_far_low, to_far_high = pack_weights((2,), (low, 3 * quarter - low), *ours)
    to_ahead, to_behind = pack_weights((1, 3), (3 * quarter,) * 2, *ours)
    (own,) = pack_weights((0,), (3 * quarter,), *ours)

    def shift(block, step):
        pairs = [
            (SIDE * y + x, SIDE * ((y + step) % SIDE) + x) for y in range(SIDE) for x in range(SIDE)
        ]
        return lax.ppermute(block, "etp", pairs)

    weights = [
        own,
        shift(to_behind, -1),
        shift(to_ahead, 1),
        shift(shift(to_far_low, 1), 1),
        shift(shift(to_far_high, -1), -1),
    ]

    came = lax.all_to_all(sent, "ep", split_axis=0, concat_axis=0, tiled=True)
    came, *weights = lax.optimization_barrier((came, *weights))
    wide = jnp.broadcast_to(came[None], (SIDE, *came.shape))
    gathered = lax.all_to_all(wide, "etp", 0, 0, tiled=True, axis_index_groups=along_x)
    gathered = jnp.swapaxes(gathered, 1, 2)

    flops = 2 * 3 * rows_all * quarter * lanes * SIDE
    part = (SIDE, 3, rows_all // 2, lanes)
    (send,) = in_vmem(
        functools.partial(forward_kernel, False), [(part, bf16)], 6, flops // 2, "forward_send"
    )(gathered, *weights)
    other = lax.ppermute(send, "ep", [(i, i ^ 1) for i in range(ep_count)])
    (keep,) = in_vmem(
        functools.partial(forward_kernel, True), [(part, jnp.float32)], 6, flops // 2, "forward_keep"
    )(gathered, *weights)
    partial = (keep + other.astype(jnp.float32)).astype(bf16)
    partial = lax.all_to_all(partial, "etp", 0, 0, tiled=True, axis_index_groups=along_y)
    pre_gate, pre_up, d_hidden = jnp.sum(partial.astype(jnp.float32), axis=0)
    sigma = jax.nn.sigmoid(pre_gate)
    d_up = (d_hidden * pre_gate * sigma).astype(bf16)
    d_gate = (d_hidden * pre_up * sigma * (1.0 + pre_gate * (1.0 - sigma))).astype(bf16)
    grads = jnp.broadcast_to(jnp.stack([d_gate, d_up])[None], (SIDE, 2, *d_up.shape))
    grads = lax.all_to_all(grads, "etp", 0, 0, tiled=True, axis_index_groups=along_y)
    grads = lax.all_gather(grads, "ep", axis_index_groups=cores)
    (back,) = in_vmem(
        backward_kernel, [((SIDE, ep_count, line), bf16)], 6, flops * 2 // 3, "backward_parts"
    )(grads, *weights)
    back = lax.all_to_all(back, "etp", 0, 0, tiled=True, axis_index_groups=along_x)
    (summed,) = in_vmem(gather_kernel, [((ep_count, 2, back_line // 2), bf16)], 1, 0, "gather_rows")(back)
    returned = lax.all_to_all(summed, "ep", split_axis=0, concat_axis=0, tiled=True)
    (result,) = in_vmem(
        combine_kernel, [((group_rows, 2 * half), bf16)], 2, 0, "combine_rows"
    )(returned.reshape(ep_count, back_line), picks)
    return result


def solution(mesh):
    return jax.shard_map(
        on_device,
        mesh=mesh,
        in_specs=(
            P("ep", "etp"),
            P("ep", "etp"),
            P("ep", None),
            P("ep", None),
            P("ep", None, "etp"),
            P("ep", None, "etp"),
            P("ep", "etp", None),
        ),
        out_specs=P("ep", "etp"),
        check_vma=False,
    )
```

```python
import functools

import jax
import jax.numpy as jnp
from jax import lax
from jax.experimental import pallas as pl
from jax.experimental.pallas import tpu as pltpu
from jax.sharding import PartitionSpec as P

SIDE = 4
STEPS = (0, 1, 3, 2)
NT = (((1,), (1,)), ((), ()))
NN = (((1,), (0,)), ((), ()))
TN = (((0,), (0,)), ((), ()))
LANES = 128
VMEM_BYTES = 24 * 1024 * 1024


def mm(a, b, dims, precision=None):
    return lax.dot_general(a, b, dims, precision=precision, preferred_element_type=jnp.float32)


def in_vmem(kernel, shapes, count, flops, name):
    return pl.pallas_call(
        kernel,
        out_shape=[jax.ShapeDtypeStruct(*shape) for shape in shapes],
        in_specs=[pl.BlockSpec(memory_space=pltpu.VMEM)] * count,
        out_specs=[pl.BlockSpec(memory_space=pltpu.VMEM)] * len(shapes),
        compiler_params=pltpu.CompilerParams(vmem_limit_bytes=VMEM_BYTES),
        cost_estimate=pl.CostEstimate(flops=flops, bytes_accessed=2_000_000, transcendentals=0),
        name=name,
    )


def pack_kernel(steps, gate_any, up_any, down_any, *rest):
    outs, sems = list(rest[:-1]), rest[-1]
    quarter = gate_any.shape[0] // SIDE
    lanes = gate_any.shape[1]
    mine = lax.axis_index("etp") // SIDE
    copies = []

    def go(source, target):
        copy = pltpu.make_async_copy(source, target, sems.at[len(copies)])
        copy.start()
        copies.append(copy)

    for step in steps:
        into = [outs.pop(0)]
        first = pl.multiple_of(lax.rem(mine + step, SIDE) * quarter, lanes)
        cut = into[0].shape[0] - quarter
        go(gate_any.at[pl.ds(first, quarter)], into[0].at[pl.ds(0, quarter)])
        if cut == 2 * quarter:
            go(up_any.at[pl.ds(first, quarter)], into[0].at[pl.ds(quarter, quarter)])
            base = 2 * quarter
        else:
            into.append(outs.pop(0))
            go(up_any.at[pl.ds(first, cut)], into[0].at[pl.ds(quarter, cut)])
            go(up_any.at[pl.ds(first + cut, quarter - cut)], into[1].at[pl.ds(0, quarter - cut)])
            base = quarter - cut
        for j in range(quarter // lanes):
            at = pl.multiple_of(first + j * lanes, lanes)
            go(down_any.at[:, pl.ds(at, lanes)], into[-1].at[pl.ds(base + j * lanes, lanes)])
    for copy in copies:
        copy.wait()


def pack_weights(steps, sizes, gate, up, down):
    lanes = gate.shape[1]
    count = len(steps) * (2 + gate.shape[0] // SIDE // lanes) + len(sizes) - len(steps)
    return pl.pallas_call(
        functools.partial(pack_kernel, steps),
        out_shape=[jax.ShapeDtypeStruct((size, lanes), gate.dtype) for size in sizes],
        in_specs=[pl.BlockSpec(memory_space=pl.ANY)] * 3,
        out_specs=[pl.BlockSpec(memory_space=pltpu.VMEM)] * len(sizes),
        scratch_shapes=[pltpu.SemaphoreType.DMA((count,))],
        compiler_params=pltpu.CompilerParams(vmem_limit_bytes=60 * 1024 * 1024),
        cost_estimate=pl.CostEstimate(flops=0, bytes_accessed=3_000_000, transcendentals=0),
        name=f"pack_{steps[0]}",
    )(gate, up, down)


def dispatch_kernel(routes_any, gates_any, tokens_any, grads_any, sent_out, picks_out, *rest):
    routes_ref, gates_ref, tokens_ref, grads_ref, sems = rest
    pairs = (
        (routes_any, routes_ref),
        (gates_any, gates_ref),
        (tokens_any, tokens_ref),
        (grads_any, grads_ref),
    )
    copies = [pltpu.make_async_copy(*pair, sems.at[n]) for n, pair in enumerate(pairs)]
    for copy in copies:
        copy.start()
    for copy in copies:
        copy.wait()
    top, group = routes_ref.shape
    capacity, sides, _ = picks_out.shape
    half = tokens_ref.shape[1] // 2
    expert = lax.broadcasted_iota(jnp.int32, (sides, group), 0) // 2
    member = jnp.zeros((sides, group), jnp.float32)
    weight = jnp.zeros((sides, group), jnp.float32)
    for k in range(top):
        named = expert == routes_ref[k : k + 1, :]
        member = jnp.where(named, 1.0, member)
        weight = jnp.where(named, gates_ref[k : k + 1, :], weight)
    earlier = lax.broadcasted_iota(jnp.int32, (group, group), 0) < lax.broadcasted_iota(
        jnp.int32, (group, group), 1
    )
    rank = mm(member, earlier.astype(jnp.float32), NN)
    even = lax.broadcasted_iota(jnp.int32, (sides, half), 0) % 2 == 0
    tokens = tokens_ref[...].astype(jnp.float32)
    grads = grads_ref[...].astype(jnp.float32)
    input_parts, grad_parts = [], []
    for s in range(capacity):
        pick = jnp.where((rank > s - 0.5) & (rank < s + 0.5), member, 0.0)
        picks_out[s] = pick
        one = mm(pick, tokens, NN)
        two = mm(pick, grads, NN) * jnp.sum(pick * weight, axis=1, keepdims=True)
        input_parts.append(jnp.where(even, one[:, :half], one[:, half:]))
        grad_parts.append(jnp.where(even, two[:, :half], two[:, half:]))
    fill = jnp.zeros((sides, sent_out.shape[2] - capacity * half), jnp.float32)
    sent_out[:, 0, :] = jnp.concatenate([*input_parts, fill], axis=1).astype(sent_out.dtype)
    sent_out[:, 1, :] = jnp.concatenate([*grad_parts, fill], axis=1).astype(sent_out.dtype)


def dispatch_rows(routes, gates, tokens, grads, capacity, sides, line):
    small = (routes, gates, tokens, grads)
    return pl.pallas_call(
        dispatch_kernel,
        out_shape=[
            jax.ShapeDtypeStruct((sides, 2, line), tokens.dtype),
            jax.ShapeDtypeStruct((capacity, sides, routes.shape[1]), jnp.float32),
        ],
        in_specs=[pl.BlockSpec(memory_space=pl.ANY)] * len(small),
        out_specs=[pl.BlockSpec(memory_space=pltpu.VMEM)] * 2,
        scratch_shapes=[
            *[pltpu.VMEM(array.shape, array.dtype) for array in small],
            pltpu.SemaphoreType.DMA((len(small),)),
        ],
        compiler_params=pltpu.CompilerParams(vmem_limit_bytes=60 * 1024 * 1024),
        cost_estimate=pl.CostEstimate(flops=0, bytes_accessed=500_000, transcendentals=0),
        name="dispatch_rows",
    )(*small)


def rows_of(parts, first, count):
    for part in parts:
        if first < part.shape[0]:
            return part[pl.ds(first, count), :]
        first -= part.shape[0]
    return None


def forward_kernel(keep, x_ref, own, ahead, behind, far_low, far_high, out_ref):
    quarter = own.shape[0] // 3
    lanes = own.shape[1]
    share = quarter // SIDE
    groups = x_ref.shape[2] // 2
    capacity = out_ref.shape[2] // groups
    mine = lax.axis_index("etp") // SIDE
    core = lax.rem(lax.axis_index("ep"), 2)
    side = core if keep else 1 - core
    here = pl.ds(pl.multiple_of(side * groups, groups), groups)

    def rows(x, which):
        return jnp.concatenate(
            [x_ref[x, which, here, s * share : (s + 1) * share] for s in range(capacity)], axis=0
        )

    inputs = [rows(x, 0) for x in range(SIDE)]
    grads = [rows(x, 1) for x in range(SIDE)]
    for step, w in zip(STEPS, ((own,), (ahead,), (behind,), (far_low, far_high))):
        place = lax.rem(mine + step, SIDE)
        down = jnp.concatenate(
            [rows_of(w, 2 * quarter + j * lanes, lanes) for j in range(quarter // lanes)], axis=1
        )
        both = None
        hidden = None
        for x in range(SIDE):
            pair = jnp.concatenate(
                [rows_of(w, x * share, share), rows_of(w, quarter + x * share, share)],
                axis=1,
            )
            one = mm(inputs[x], pair, NN)
            two = mm(grads[x], down[:, x * share : (x + 1) * share], NT)
            both = one if both is None else both + one
            hidden = two if hidden is None else hidden + two
        out_ref[place, 0] = both[:, :lanes].astype(out_ref.dtype)
        out_ref[place, 1] = both[:, lanes:].astype(out_ref.dtype)
        out_ref[place, 2] = hidden.astype(out_ref.dtype)


def backward_kernel(d_ref, own, ahead, behind, far_low, far_high, out_ref):
    quarter = own.shape[0] // 3
    share = quarter // SIDE
    groups = out_ref.shape[1] // 2
    rows = d_ref.shape[3]
    mine = lax.axis_index("etp") // SIDE
    grads = []
    for step in STEPS:
        place = lax.rem(mine + step, SIDE)
        grads.append(
            jnp.concatenate(
                [
                    jnp.concatenate([d_ref[side, place, 0], d_ref[side, place, 1]], axis=1)
                    for side in range(2)
                ],
                axis=0,
            )
        )
    fill = jnp.zeros((groups, out_ref.shape[2] - rows // groups * share), jnp.float32)
    for x in range(SIDE):
        total = None
        for grad, w in zip(grads, ((own,), (ahead,), (behind,), (far_low, far_high))):
            pair = jnp.concatenate(
                [rows_of(w, x * share, share), rows_of(w, quarter + x * share, share)], axis=1
            )
            one = mm(grad, pair, NT)
            total = one if total is None else total + one
        for side in range(2):
            blocks = [
                total[side * rows + s * groups : side * rows + (s + 1) * groups]
                for s in range(rows // groups)
            ]
            line = jnp.concatenate([*blocks, fill], axis=1)
            out_ref[x, pl.ds(side * groups, groups), :] = line.astype(out_ref.dtype)


def gather_kernel(parts_ref, out_ref):
    width = out_ref.shape[2]
    total = parts_ref[0].astype(jnp.float32)
    for x in range(1, SIDE):
        total = total + parts_ref[x].astype(jnp.float32)
    fill = jnp.zeros((total.shape[0], 2 * width - total.shape[1]), jnp.float32)
    line = jnp.concatenate([total, fill], axis=1).astype(out_ref.dtype)
    out_ref[:, 0, :] = line[:, :width]
    out_ref[:, 1, :] = line[:, width:]


def combine_kernel(came_ref, picks_ref, out_ref):
    capacity, sides, group = picks_ref.shape
    half = out_ref.shape[1] // 2
    odd = lax.broadcasted_iota(jnp.int32, (sides, group), 0) % 2
    totals = [None, None]
    for s in range(capacity):
        block = came_ref[:, s * half : (s + 1) * half].astype(jnp.float32)
        for side in range(2):
            one = mm(jnp.where(odd == side, picks_ref[s], 0.0), block, TN)
            totals[side] = one if totals[side] is None else totals[side] + one
    out_ref[...] = jnp.concatenate(totals, axis=1).astype(out_ref.dtype)


def on_device(tokens, grad_out, routes, route_gates, gate_weight, up_weight, down_weight):
    bf16 = jnp.bfloat16
    ep_count = lax.axis_size("ep")
    experts = ep_count // 2
    group_rows, top_count = routes.shape
    capacity = min(group_rows, 5 * group_rows * top_count // (4 * experts))
    half = tokens.shape[1] // 2
    rows_all = ep_count * capacity
    lanes = gate_weight.shape[2]
    quarter = gate_weight.shape[1] // SIDE
    line = -(-capacity * half // LANES) * LANES
    back_line = -(-capacity * half // (2 * LANES)) * 2 * LANES
    along_x = [[SIDE * y + x for x in range(SIDE)] for y in range(SIDE)]
    along_y = [[SIDE * y + x for y in range(SIDE)] for x in range(SIDE)]
    cores = [[2 * z, 2 * z + 1] for z in range(experts)]

    sent, picks = dispatch_rows(
        routes.T, route_gates.T, tokens, grad_out, capacity, ep_count, line
    )
    ours = (gate_weight[0], up_weight[0], down_weight[0])
    low = quarter + quarter // 2
    to_far_low, to_far_high = pack_weights((2,), (low, 3 * quarter - low), *ours)
    to_ahead, to_behind = pack_weights((1, 3), (3 * quarter,) * 2, *ours)
    (own,) = pack_weights((0,), (3 * quarter,), *ours)

    def shift(block, step):
        pairs = [
            (SIDE * y + x, SIDE * ((y + step) % SIDE) + x) for y in range(SIDE) for x in range(SIDE)
        ]
        return lax.ppermute(block, "etp", pairs)

    weights = [
        own,
        shift(to_behind, -1),
        shift(to_ahead, 1),
        shift(shift(to_far_low, 1), 1),
        shift(shift(to_far_high, -1), -1),
    ]

    came = lax.all_to_all(sent, "ep", split_axis=0, concat_axis=0, tiled=True)
    came, *weights = lax.optimization_barrier((came, *weights))
    wide = jnp.broadcast_to(came[None], (SIDE, *came.shape))
    gathered = lax.all_to_all(wide, "etp", 0, 0, tiled=True, axis_index_groups=along_x)
    gathered = jnp.swapaxes(gathered, 1, 2)

    flops = 2 * 3 * rows_all * quarter * lanes * SIDE
    part = (SIDE, 3, rows_all // 2, lanes)
    (send,) = in_vmem(
        functools.partial(forward_kernel, False), [(part, bf16)], 6, flops // 2, "forward_send"
    )(gathered, *weights)
    other = lax.ppermute(send, "ep", [(i, i ^ 1) for i in range(ep_count)])
    (keep,) = in_vmem(
        functools.partial(forward_kernel, True), [(part, jnp.float32)], 6, flops // 2, "forward_keep"
    )(gathered, *weights)
    partial = (keep + other.astype(jnp.float32)).astype(bf16)
    partial = lax.all_to_all(partial, "etp", 0, 0, tiled=True, axis_index_groups=along_y)
    pre_gate, pre_up, d_hidden = jnp.sum(partial.astype(jnp.float32), axis=0)
    sigma = jax.nn.sigmoid(pre_gate)
    d_up = (d_hidden * pre_gate * sigma).astype(bf16)
    d_gate = (d_hidden * pre_up * sigma * (1.0 + pre_gate * (1.0 - sigma))).astype(bf16)
    grads = jnp.broadcast_to(jnp.stack([d_gate, d_up])[None], (SIDE, 2, *d_up.shape))
    grads = lax.all_to_all(grads, "etp", 0, 0, tiled=True, axis_index_groups=along_y)
    grads = lax.all_gather(grads, "ep", axis_index_groups=cores)
    (back,) = in_vmem(
        backward_kernel, [((SIDE, ep_count, line), bf16)], 6, flops * 2 // 3, "backward_parts"
    )(grads, *weights)
    back = lax.all_to_all(back, "etp", 0, 0, tiled=True, axis_index_groups=along_x)
    (summed,) = in_vmem(gather_kernel, [((ep_count, 2, back_line // 2), bf16)], 1, 0, "gather_rows")(back)
    returned = lax.all_to_all(summed, "ep", split_axis=0, concat_axis=0, tiled=True)
    (result,) = in_vmem(
        combine_kernel, [((group_rows, 2 * half), bf16)], 2, 0, "combine_rows"
    )(returned.reshape(ep_count, back_line), picks)
    return result


def solution(mesh):
    return jax.shard_map(
        on_device,
        mesh=mesh,
        in_specs=(
            P("ep", "etp"),
            P("ep", "etp"),
            P("ep", None),
            P("ep", None),
            P("ep", None, "etp"),
            P("ep", None, "etp"),
            P("ep", "etp", None),
        ),
        out_specs=P("ep", "etp"),
        check_vma=False,
    )
```
